512 devices in a mesh: ex: 8 (over y, core), par: 64 (over x, z).
Axes of the slice: x: 4, y: 4, z: 16, core: 2. Of those that a mesh axis runs over, the one named last changes fastest.
Arguments:
- activations: bfloat16 [16, 512, 16384], P('ex', None, 'par'), may hold values from -6 to 6
- out_grads: bfloat16 [16, 512, 4096], P('ex', None, 'par'), may hold values from -0.25 to 0.25
- sign_words: int32 [4096, 1024], P(None, 'par'), may hold values from 0 to 65535
- indices: int32 [8192], replicated, may hold values from 0 to 67108863, as said below
Outputs:
- sketch: float32 [16, 8192], P('ex', 'par')
The draws below stay inside these ranges and needn't reach their ends.
Inputs may be any that keep to these rules, and one draw needn't show every extreme that they name: `indices`: entries 128 q to 128 q + 127 are increasing and distinct and lie in [q * 1048576, (q + 1) * 1048576); the first entry is 0 and the last is 67108863.
All inputs are finite; a program needn't handle non-finite values.
Results may differ from the reference program's by a relative error of at most 0.0029.
Values may be sent and summed in bfloat16 or wider, within the bound.
No kernel may reach another device: no remote copies, remote signals or barrier semaphores. Data moves between devices by JAX's collectives and lax.ppermute only.
A program may use at most 64 MiB of HBM per device.

```python
import math
import jax
import jax.numpy as jnp
from jax import lax

D = 4096
FF = 16384
TOK = 512
KDEV = 128
EXAMPLES = 16
KTOTAL = 8192
REGION = 1048576
N_PAR = 64


def draw_indices(key, part):
    key = jax.random.fold_in(key, 7)
    position = jnp.arange(KTOTAL, dtype=jnp.int32)
    block_idx = position // KDEV
    within = position % KDEV
    stratum = REGION // KDEV
    offset = jax.random.randint(key, (KTOTAL,), 0, stratum, dtype=jnp.int32)
    result = block_idx * REGION + within * stratum + offset
    result = jnp.where(position == 0, 0, result)
    result = jnp.where(position == KTOTAL - 1, D * FF - 1, result)
    return result.astype(jnp.int32)


def plant(entries, rng, smallest, high):
    shape = entries.shape
    place = [jax.random.randint(jax.random.fold_in(rng, axis), (), 0, shape[axis]) for axis in range(len(shape))]
    entries = entries.at[tuple(place)].set(smallest)
    longest = shape.index(max(shape))
    place[longest] = (place[longest] + 1) % shape[longest]
    return entries.at[tuple(place)].set(high)


def steps_of(key, extent, pieces, smallest, high):
    def one(dim, shards_of):
        heights = jax.random.uniform(jax.random.fold_in(jax.random.fold_in(key, 6), dim), (shards_of,), jnp.float32, smallest / len(pieces), high / len(pieces))
        return jnp.repeat(jnp.exp(heights), extent[dim] // shards_of).reshape((-1,) + (1,) * (len(extent) - dim - 1))

    level = one(*pieces[0])
    for cut in pieces[1:]:
        level = level * one(*cut)
    return level


def normal_values(key, dims, scale, limit, cuts=(), kind=jnp.bfloat16):
    level = steps_of(key, dims, cuts, -0.22, 0.18) if cuts else 1.0
    array = jax.random.normal(key, dims, jnp.float32) * scale * level
    return jnp.minimum(jnp.maximum(array, -limit), limit).astype(kind)


def setup_inputs(seed: int = 0) -> dict:
    key_of = jax.random.split(jax.random.key(seed), 5)
    return {
        "activations": normal_values(key_of[0], (EXAMPLES, TOK, FF), 1.0, 6.0, ((0, 8), (2, 64))),
        "out_grads": normal_values(key_of[1], (EXAMPLES, TOK, D), TOK ** -0.5, 0.25, ((0, 8), (2, 64))),
        "sign_words": plant(jax.random.randint(key_of[2], (D, FF // 16), 0, 65536), jax.random.fold_in(key_of[2], 1), 0, 65535).astype(jnp.int32),
        "indices": draw_indices(jax.random.fold_in(key_of[4], 71), 0),
    }


def parity_sign(values, matrix_order):
    bit_count = jnp.zeros(values.shape, jnp.int32)
    for bit_level in range(matrix_order.bit_length() - 1):
        bit_count = bit_count + jnp.bitwise_and(jnp.right_shift(values, bit_level), 1)
    return (1 - 2 * (bit_count % 2)).astype(jnp.float32)

def hadamard_matrix(matrix_order):
    row_ids = jnp.arange(matrix_order, dtype=jnp.int32)[:, None]
    col_ids = jnp.arange(matrix_order, dtype=jnp.int32)[None, :]
    return parity_sign(jnp.bitwise_and(row_ids, col_ids), matrix_order)

def unpack_signs(packed):
    shifts = jnp.arange(16, dtype=jnp.int32)
    bitset = jnp.bitwise_and(jnp.right_shift(packed[:, :, None], shifts), 1)
    return (1 - 2 * bitset).astype(jnp.float32).reshape(packed.shape[0], packed.shape[1] * 16)

def factor_list(matrix_order):
    factors = []
    while matrix_order > 1:
        factor = min(matrix_order, 16)
        factors.append(factor)
        matrix_order = matrix_order // factor
    return factors

def transform_axis(values, axis_pos, matrix_order):
    old_shape = values.shape
    factors = factor_list(matrix_order)
    values = values.reshape(old_shape[:axis_pos] + tuple(factors) + old_shape[axis_pos + 1:])
    for position, factor in enumerate(factors):
        values = jnp.tensordot(hadamard_matrix(factor), values, axes=((1,), (axis_pos + position,)), precision=lax.Precision.HIGHEST)
        values = jnp.moveaxis(values, 0, axis_pos + position)
    return values.reshape(old_shape)

def reference(activations, out_grads, sign_words, indices):
    sign_values = unpack_signs(sign_words)
    local_cols = FF // N_PAR
    norm_scale = 1.0 / math.sqrt(D * FF)
    row_idx = indices // FF
    column = indices % FF
    block_idx = column // local_cols
    within = column % local_cols
    flip_signs = parity_sign(jnp.bitwise_and(block_idx[:, None], jnp.arange(N_PAR, dtype=jnp.int32)[None, :]), N_PAR)

    def one_example(example_pair):
        example_acts, grad_rows = example_pair
        gradient = lax.dot_general(grad_rows, example_acts, (((0,), (0,)), ((), ())), preferred_element_type=jnp.float32)
        signed = (gradient * sign_values).reshape(D, N_PAR, local_cols)
        transformed = transform_axis(signed, 0, D)
        transformed = transform_axis(transformed, 2, local_cols)
        partial_value = (transformed * norm_scale).astype(jnp.bfloat16)
        picked = partial_value[row_idx, :, within].astype(jnp.float32)
        return lax.optimization_barrier(jnp.sum(picked * flip_signs, axis=1))
    sketch = lax.map(one_example, (activations, out_grads))
    return sketch - lax.optimization_barrier(jnp.mean(sketch, axis=0, keepdims=True))
```

```python
import jax
import jax.numpy as jnp
from jax import lax
from jax.experimental import pallas as pl
from jax.experimental.pallas import tpu as pltpu
from jax.sharding import Mesh, PartitionSpec as P

D = 4096
FF = 16384
TOK = 512
NX = 4
NZ = 16
ROWS = D // NX
COLS = 256
LOW = 64
TILES = ROWS // LOW
KDEV = 128
SAMPLES = NX * KDEV
WIRE = 131072.0
SCALE = 1.0 / 8192.0 / WIRE
VMEM_BYTES = 56 * 1024 * 1024


def sign_of(bits):
    bits = bits ^ (bits >> 4)
    bits = bits ^ (bits >> 2)
    bits = bits ^ (bits >> 1)
    return (1 - 2 * (bits & 1)).astype(jnp.float32)


def prep_kernel(pos_ref, idx_ref, w0, w1, w2, w3, had_ref, hs_ref, js_ref, sign_ref):
    x, z = pos_ref[0], pos_ref[1]
    row = lax.broadcasted_iota(jnp.int32, (COLS, 2 * COLS), 0)
    col = lax.broadcasted_iota(jnp.int32, (COLS, 2 * COLS), 1) & (COLS - 1)
    had_ref[...] = sign_of(row & col).astype(jnp.bfloat16)

    def tile_body(tile, carry):
        idx = idx_ref[pl.ds(tile, 1), :]
        line = lax.broadcasted_iota(jnp.int32, (16, SAMPLES), 0)
        low_signs = sign_of(line & idx)
        high_signs = sign_of(line & (idx >> 4))
        for a in range(16):
            block_rows = low_signs * high_signs[a : a + 1]
            hs_ref[tile, pl.ds(16 * a, 16), :] = block_rows.astype(jnp.bfloat16)
        block = lax.broadcasted_iota(jnp.int32, (NX, SAMPLES), 0)
        sx = (idx >> 12) & 3
        sz = (idx >> 8) & 15
        tx = (idx >> 24) & 3
        js_ref[tile] = sign_of((block & sx) | ((sz & z) << 2) | ((tx & x) << 6)) * SCALE
        return carry

    lax.fori_loop(0, TILES, tile_body, 0)

    byte_row = lax.broadcasted_iota(jnp.int32, (32, COLS), 0)
    byte_col = lax.broadcasted_iota(jnp.int32, (32, COLS), 1)
    spread = (byte_row == (byte_col >> 4) + 16 * ((byte_col >> 3) & 1)).astype(jnp.float32)
    spread = spread.astype(jnp.bfloat16)
    shift = lax.broadcasted_iota(jnp.int32, (ROWS, COLS), 1) & 7
    for delta, w_ref in enumerate((w0, w1, w2, w3)):
        words = w_ref[...]
        two = jnp.concatenate([words & 255, (words >> 8) & 255], axis=0)
        two = two.astype(jnp.float32).astype(jnp.bfloat16)
        value = lax.dot_general(
            two, spread, (((0,), (0,)), ((), ())), preferred_element_type=jnp.float32
        )
        bit = (value.astype(jnp.int32) >> shift) & 1
        sign_ref[x ^ delta] = (1 - 2 * bit).astype(jnp.float32).astype(jnp.bfloat16)


def split(values):
    high = values.astype(jnp.bfloat16)
    return high, (values - high.astype(jnp.float32)).astype(jnp.bfloat16)


def main_kernel(
    pos_ref, idx_ref, js_ref, had_ref, grads_in, acts_in, sign_in, hs_in,
    out_ref, grads, acts, signs, hs, tiles, grad_sem, act_sem, sign_sem, hs_sem,
):
    def load(source, target, sem):
        pltpu.make_async_copy(source, target, sem).start()

    for example in range(2):
        load(grads_in.at[:, example], grads.at[example], grad_sem.at[example])
        for block in range(NX):
            load(acts_in.at[block, example], acts.at[example, block], act_sem.at[example, block])
            if example == 0:
                load(sign_in.at[block], signs.at[block], sign_sem.at[block])
        if example == 0:
            load(hs_in, hs, hs_sem)

    def wait(target, sem):
        pltpu.make_async_copy(target, target, sem).wait()

    had = had_ref[...]
    for example in range(2):
        wait(grads.at[example], grad_sem.at[example])

        def block_body(block, carry, example=example):
            wait(acts.at[example, block], act_sem.at[example, block])
            if example == 0:
                wait(signs.at[block], sign_sem.at[block])
            grad = jnp.dot(
                grads[example].reshape(ROWS, TOK),
                acts[example, block],
                preferred_element_type=jnp.float32,
            )
            signed = grad * signs[block].astype(jnp.float32)
            parts = []
            for b in range(4):
                both = jnp.concatenate(split(signed[b * COLS : (b + 1) * COLS]), axis=0)
                parts.append(jnp.dot(had, both, preferred_element_type=jnp.float32))
            p0, p1 = parts[0] + parts[1], parts[0] - parts[1]
            p2, p3 = parts[2] + parts[3], parts[2] - parts[3]
            for a, value in enumerate((p0 + p2, p1 + p3, p0 - p2, p1 - p3)):
                value = value.astype(jnp.bfloat16)
                for i in range(4):
                    tiles[4 * a + i, example, block] = value[i * LOW : (i + 1) * LOW]
            return carry

        lax.fori_loop(0, NX, block_body, 0)

    wait(hs, hs_sem)

    def tile_body(tile, carry):
        low_row = (idx_ref[pl.ds(tile, 1), :] >> 14) & (LOW - 1)
        chosen = lax.broadcasted_iota(jnp.int32, (LOW, SAMPLES), 0) == low_row
        weights = js_ref[tile]
        left = tiles[tile].reshape(2 * NX * LOW, COLS)
        both = jnp.dot(left, hs[tile], preferred_element_type=jnp.float32)
        for example in range(2):
            total = jnp.zeros((LOW, SAMPLES), jnp.float32)
            for j in range(NX):
                start = (example * NX + j) * LOW
                total = total + both[start : start + LOW] * weights[j : j + 1]
            picked = jnp.sum(jnp.where(chosen, total, 0.0), axis=0, keepdims=True)
            for tx in range(NX):
                out_ref[tile, tx, pl.ds(example, 1), :] = picked[:, tx * KDEV : (tx + 1) * KDEV]
        return carry

    lax.fori_loop(0, TILES, tile_body, 0)


def shards(activations, out_grads, sign_words, indices):
    ex_size = lax.axis_size("ex")
    x, z = lax.axis_index("x"), lax.axis_index("z")
    position = jnp.stack([x, z]).astype(jnp.int32)

    acts = lax.all_gather(activations, "x", axis=0, tiled=False)

    wire = jnp.transpose(out_grads, (0, 2, 1)).astype(jnp.float32) * WIRE
    wire = lax.all_gather(wire.astype(jnp.float16), "z", axis=0, tiled=False)
    grads = wire.astype(jnp.float32).astype(jnp.bfloat16)

    words = jnp.transpose(sign_words, (1, 0)).reshape(FF // 1024, NX, ROWS)
    own_words = []
    for delta in range(NX):
        part = lax.dynamic_index_in_dim(words, x ^ delta, axis=1, keepdims=False)
        if delta:
            part = lax.ppermute(part, "x", [(i, i ^ delta) for i in range(NX)])
        own_words.append(part)
    order = indices.reshape(NX, TILES, KDEV).transpose(1, 0, 2).reshape(TILES, SAMPLES)
    vmem = pl.BlockSpec(memory_space=pltpu.VMEM)
    smem = pl.BlockSpec(memory_space=pltpu.SMEM)
    anywhere = pl.BlockSpec(memory_space=pl.ANY)
    had, hs, js, signs = pl.pallas_call(
        prep_kernel,
        out_shape=[
            jax.ShapeDtypeStruct((COLS, 2 * COLS), jnp.bfloat16),
            jax.ShapeDtypeStruct((TILES, COLS, SAMPLES), jnp.bfloat16),
            jax.ShapeDtypeStruct((TILES, NX, SAMPLES), jnp.float32),
            jax.ShapeDtypeStruct((NX, ROWS, COLS), jnp.bfloat16),
        ],
        in_specs=[smem] + [vmem] * 5,
        out_specs=[vmem] * 4,
        compiler_params=pltpu.CompilerParams(vmem_limit_bytes=VMEM_BYTES),
        cost_estimate=pl.CostEstimate(
            flops=40 * 1024 * 1024, bytes_accessed=8 * 1024 * 1024, transcendentals=0
        ),
        name="prepare_signs",
    )(position, order, *own_words)

    values = pl.pallas_call(
        main_kernel,
        out_shape=jax.ShapeDtypeStruct((TILES, NX, 2, KDEV), jnp.float32),
        in_specs=[smem] + [vmem] * 3 + [anywhere] * 4,
        out_specs=vmem,
        scratch_shapes=[
            pltpu.VMEM((2, NZ, LOW, TOK), jnp.bfloat16),
            pltpu.VMEM((2, NX, TOK, COLS), jnp.bfloat16),
            pltpu.VMEM((NX, ROWS, COLS), jnp.bfloat16),
            pltpu.VMEM((TILES, COLS, SAMPLES), jnp.bfloat16),
            pltpu.VMEM((TILES, 2, NX, LOW, COLS), jnp.bfloat16),
            pltpu.SemaphoreType.DMA((2,)),
            pltpu.SemaphoreType.DMA((2, NX)),
            pltpu.SemaphoreType.DMA((NX,)),
            pltpu.SemaphoreType.DMA,
        ],
        compiler_params=pltpu.CompilerParams(vmem_limit_bytes=VMEM_BYTES),
        cost_estimate=pl.CostEstimate(
            flops=7 * 10**9, bytes_accessed=16 * 1024 * 1024, transcendentals=0
        ),
        name="gradient_transform_sample",
    )(position, order, js, had, grads, acts, signs, hs)

    along_z = lax.all_to_all(values, "z", split_axis=0, concat_axis=0, tiled=True)
    half = jnp.sum(along_z, axis=0)
    sent = jnp.broadcast_to(half[None], (ex_size, NX, 2, KDEV)).reshape(ex_size * NX, 2, KDEV)
    received = lax.all_to_all(sent, ("ex", "x"), split_axis=0, concat_axis=0, tiled=True)
    raw = jnp.sum(received.reshape(ex_size, NX, 2, KDEV), axis=1)
    own_raw = lax.dynamic_index_in_dim(raw, lax.axis_index("ex"), axis=0, keepdims=False)
    return own_raw - jnp.sum(raw, axis=(0, 1))[None, :] / (2 * ex_size)


def solution(mesh):
    ex_size = mesh.shape["ex"]
    grid = Mesh(mesh.devices.reshape(ex_size, NX, NZ), ("ex", "x", "z"))
    return jax.shard_map(
        shards,
        mesh=grid,
        in_specs=(P("ex", None, ("x", "z")), P("ex", None, ("x", "z")), P(None, ("x", "z")), P()),
        out_specs=P("ex", ("x", "z")),
        check_vma=False,
    )
```

```python
import jax
import jax.numpy as jnp
from jax import lax
from jax.experimental import pallas as pl
from jax.experimental.pallas import tpu as pltpu
from jax.sharding import Mesh, PartitionSpec as P

D = 4096
FF = 16384
TOK = 512
NX = 4
NZ = 16
ROWS = D // NX
COLS = 256
LOW = 64
TILES = ROWS // LOW
KDEV = 128
SAMPLES = NX * KDEV
WIRE = 131072.0
SCALE = 1.0 / 8192.0 / WIRE
VMEM_BYTES = 56 * 1024 * 1024


def sign_of(bits):
    bits = bits ^ (bits >> 4)
    bits = bits ^ (bits >> 2)
    bits = bits ^ (bits >> 1)
    return (1 - 2 * (bits & 1)).astype(jnp.float32)


def split(values):
    high = values.astype(jnp.bfloat16)
    return high, (values - high.astype(jnp.float32)).astype(jnp.bfloat16)


def main_kernel(
    idx_ref, w0, w1, w2, w3, grads_in, acts_in,
    out_ref, grads, acts, words, signs, tiles, grad_sem, act_sem,
):
    x, z = lax.axis_index("x"), lax.axis_index("z")
    flip = lax.axis_index("core") * (NZ - 1)

    def load(source, target, sem):
        pltpu.make_async_copy(source, target, sem).start()

    def wait(target, sem):
        pltpu.make_async_copy(target, target, sem).wait()

    for example in range(2):
        for i in range(NZ):
            load(grads_in.at[i ^ flip, example], grads.at[example, i], grad_sem.at[example, i])
        load(acts_in.at[0, example], acts.at[example, 0], act_sem.at[example, 0])
    for block in range(1, NX):
        for example in range(2):
            load(acts_in.at[block, example], acts.at[example, block], act_sem.at[example, block])

    row = lax.broadcasted_iota(jnp.int32, (COLS, COLS), 0)
    col = lax.broadcasted_iota(jnp.int32, (COLS, COLS), 1)
    had = sign_of(row & col).astype(jnp.bfloat16)
    had = jnp.concatenate([had, had], axis=1)
    byte_row = lax.broadcasted_iota(jnp.int32, (32, COLS), 0)
    byte_col = lax.broadcasted_iota(jnp.int32, (32, COLS), 1)
    spread = (byte_row == (byte_col >> 4) + 16 * ((byte_col >> 3) & 1)).astype(jnp.float32)
    spread = spread.astype(jnp.bfloat16)
    for delta, w_ref in enumerate((w0, w1, w2, w3)):
        words[x ^ delta] = w_ref[...]

    for example in range(2):
        for i in range(NZ):
            wait(grads.at[example, i], grad_sem.at[example, i])

    def block_body(block, carry):
        word = words[block]
        two = jnp.concatenate([word & 255, (word >> 8) & 255], axis=0)
        two = two.astype(jnp.float32).astype(jnp.bfloat16)
        value = lax.dot_general(
            two, spread, (((0,), (0,)), ((), ())), preferred_element_type=jnp.float32
        )
        shift = lax.broadcasted_iota(jnp.int32, (ROWS, COLS), 1) & 7
        signs[block] = (1 - 2 * ((value.astype(jnp.int32) >> shift) & 1)).astype(jnp.float32)
        for example in range(2):
            wait(acts.at[example, block], act_sem.at[example, block])
            grad = jnp.dot(
                grads[example].reshape(ROWS, TOK),
                acts[example, block],
                preferred_element_type=jnp.float32,
            )
            signed = grad * signs[block]
            parts = []
            for b in range(4):
                both = jnp.concatenate(split(signed[b * COLS : (b + 1) * COLS]), axis=0)
                parts.append(jnp.dot(had, both, preferred_element_type=jnp.float32))
            p0, p1 = parts[0] + parts[1], parts[0] - parts[1]
            p2, p3 = parts[2] + parts[3], parts[2] - parts[3]
            for a, value in enumerate((p0 + p2, p1 + p3, p0 - p2, p1 - p3)):
                value = value.astype(jnp.bfloat16)
                for i in range(4):
                    tiles[4 * a + i, example, block] = value[i * LOW : (i + 1) * LOW]
        return carry

    lax.fori_loop(0, NX, block_body, 0, unroll=True)

    def tile_body(tile, carry):
        idx = jnp.concatenate([idx_ref[pl.ds(tx * NZ + tile, 1), :] for tx in range(NX)], axis=1)
        line = lax.broadcasted_iota(jnp.int32, (16, SAMPLES), 0)
        low_signs = sign_of(line & idx)
        high_signs = sign_of(line & (idx >> 4))
        weights = jnp.concatenate(
            [(low_signs * high_signs[a : a + 1]).astype(jnp.bfloat16) for a in range(16)], axis=0
        )
        sign_z = sign_of((idx >> 8) & 15 & z)
        sign_1 = sign_of((idx >> 12) & 1)
        sign_2 = sign_of((idx >> 13) & 1)
        chosen = lax.broadcasted_iota(jnp.int32, (LOW, SAMPLES), 0) == ((idx >> 14) & (LOW - 1))
        left = tiles[tile].reshape(2 * NX * LOW, COLS)
        both = jnp.dot(left, weights, preferred_element_type=jnp.float32)
        for example in range(2):
            b0, b1, b2, b3 = [
                both[(example * NX + j) * LOW : (example * NX + j + 1) * LOW] for j in range(NX)
            ]
            total = (b0 + b1 * sign_1) + (b2 + b3 * sign_1) * sign_2
            picked = jnp.sum(jnp.where(chosen, total, 0.0), axis=0, keepdims=True) * sign_z
            for tx in range(NX):
                out_ref[tile, tx, pl.ds(example, 1), :] = picked[:, tx * KDEV : (tx + 1) * KDEV]
        return carry

    lax.fori_loop(0, TILES, tile_body, 0, unroll=4)


def shards(activations, out_grads, sign_words, indices):
    ex = ("y", "core")
    ex_size = lax.axis_size(ex)
    x = lax.axis_index("x")

    acts = lax.all_gather(activations, "x", axis=0, tiled=False)

    words = jnp.transpose(sign_words, (1, 0))
    own_words = []
    for delta in range(NX):
        part = lax.dynamic_slice_in_dim(words, (x ^ delta) * ROWS, ROWS, axis=1)
        if delta:
            part = lax.ppermute(part, "x", [(i, i ^ delta) for i in range(NX)])
        own_words.append(part)

    wire = jnp.transpose(out_grads, (0, 2, 1)).astype(jnp.float32) * WIRE
    wire = lax.all_gather(
        wire.astype(jnp.float16), ("core", "z"), axis=0, tiled=False,
        axis_index_groups=[list(range(NZ)), list(range(2 * NZ - 1, NZ - 1, -1))],
    )
    grads = wire.astype(jnp.float32).astype(jnp.bfloat16)

    vmem = pl.BlockSpec(memory_space=pltpu.VMEM)
    anywhere = pl.BlockSpec(memory_space=pl.ANY)
    values = pl.pallas_call(
        main_kernel,
        out_shape=jax.ShapeDtypeStruct((TILES, NX, 2, KDEV), jnp.float32),
        in_specs=[vmem] * 5 + [anywhere] * 2,
        out_specs=vmem,
        scratch_shapes=[
            pltpu.VMEM((2, NZ, LOW, TOK), jnp.bfloat16),
            pltpu.VMEM((2, NX, TOK, COLS), jnp.bfloat16),
            pltpu.VMEM((NX, FF // 1024, ROWS), jnp.int32),
            pltpu.VMEM((NX, ROWS, COLS), jnp.float32),
            pltpu.VMEM((TILES, 2, NX, LOW, COLS), jnp.bfloat16),
            pltpu.SemaphoreType.DMA((2, NZ)),
            pltpu.SemaphoreType.DMA((2, NX)),
        ],
        compiler_params=pltpu.CompilerParams(vmem_limit_bytes=VMEM_BYTES),
        cost_estimate=pl.CostEstimate(
            flops=7 * 10**9, bytes_accessed=8 * 1024 * 1024, transcendentals=0
        ),
        name="gradient_transform_sample",
    )(indices.reshape(NX * NZ, KDEV), *own_words, grads, acts)

    along_z = lax.all_to_all(values, "z", split_axis=0, concat_axis=0, tiled=True)
    own_indices = lax.dynamic_index_in_dim(
        indices.reshape(NX, NZ, KDEV), lax.axis_index("z"), axis=1, keepdims=False
    )
    half = jnp.sum(along_z, axis=0) * (sign_of((own_indices >> 24) & x) * SCALE)[:, None, :]
    sent = jnp.broadcast_to(half[None], (ex_size, NX, 2, KDEV)).reshape(ex_size * NX, 2, KDEV)
    received = lax.all_to_all(sent, ex + ("x",), split_axis=0, concat_axis=0, tiled=True)
    raw = jnp.sum(received.reshape(ex_size, NX, 2, KDEV), axis=1)
    own_raw = lax.dynamic_index_in_dim(raw, lax.axis_index(ex), axis=0, keepdims=False)
    return own_raw - jnp.sum(raw, axis=(0, 1))[None, :] / (2 * ex_size)


def solution(mesh):
    grid = Mesh(mesh.devices.reshape(-1, 2, NX, NZ), ("y", "core", "x", "z"))
    ex, par = ("y", "core"), ("x", "z")
    return jax.shard_map(
        shards,
        mesh=grid,
        in_specs=(P(ex, None, par), P(ex, None, par), P(None, par), P()),
        out_specs=P(ex, par),
        check_vma=False,
    )
```

```python
import jax
import jax.numpy as jnp
from jax import lax
from jax.experimental import pallas as pl
from jax.experimental.pallas import tpu as pltpu
from jax.sharding import Mesh, PartitionSpec as P

D = 4096
FF = 16384
TOK = 512
NX = 4
NZ = 16
Z = ("zh", "zl")
ROWS = D // NX
COLS = 256
LOW = 64
TILES = ROWS // LOW
KDEV = 128
SAMPLES = NX * KDEV
WIRE = 131072.0
SCALE = 1.0 / 8192.0 / WIRE
VMEM_BYTES = 36 * 1024 * 1024


def sign_of(bits):
    bits = bits ^ (bits >> 4)
    bits = bits ^ (bits >> 2)
    bits = bits ^ (bits >> 1)
    return (1 - 2 * (bits & 1)).astype(jnp.float32)


def split(values):
    high = values.astype(jnp.bfloat16)
    return high, (values - high.astype(jnp.float32)).astype(jnp.bfloat16)


def pack_kernel(acts_ref, words_ref, own_ref, *payloads):
    x = lax.axis_index("x")
    for delta, ref in enumerate((own_ref,) + payloads):
        start = pl.multiple_of((x ^ delta) * ROWS, ROWS)
        word = words_ref[:, pl.ds(start, ROWS)]
        two = jnp.concatenate([word & 255, (word >> 8) & 255], axis=0)
        two = two.astype(jnp.float32).astype(jnp.bfloat16)
        first = 2 * TOK if delta else 0
        for q in range(4):
            ref[pl.ds(first + 32 * q, 32), :] = two[:, q * COLS : (q + 1) * COLS]
        if delta:
            for example in range(2):
                ref[pl.ds(example * TOK, TOK), :] = acts_ref[example]


def main_kernel(idx_ref, grads, own_bytes, own_acts, p1, p2, p3, out_ref, signs, tiles):
    x, z = lax.axis_index("x"), lax.axis_index(Z)

    row = lax.broadcasted_iota(jnp.int32, (COLS, COLS), 0)
    col = lax.broadcasted_iota(jnp.int32, (COLS, COLS), 1)
    had = sign_of(row & col).astype(jnp.bfloat16)
    had = jnp.concatenate([had, had], axis=1)
    byte_row = lax.broadcasted_iota(jnp.int32, (32, COLS), 0)
    byte_col = lax.broadcasted_iota(jnp.int32, (32, COLS), 1)
    spread = (byte_row == (byte_col >> 4) + 16 * ((byte_col >> 3) & 1)).astype(jnp.float32)
    spread = spread.astype(jnp.bfloat16)
    shift = lax.broadcasted_iota(jnp.int32, (COLS, COLS), 1) & 7

    for delta, payload in enumerate((None, p1, p2, p3)):
        block = x ^ delta
        for q in range(4):
            if delta:
                two = payload[pl.ds(2 * TOK + 32 * q, 32), :]
            else:
                two = own_bytes[pl.ds(32 * q, 32), :]
            value = lax.dot_general(
                two, spread, (((0,), (0,)), ((), ())), preferred_element_type=jnp.float32
            )
            bit = (value.astype(jnp.int32) >> shift) & 1
            signs[delta, pl.ds(q * COLS, COLS), :] = (1 - 2 * bit).astype(jnp.float32)
        for example in range(2):
            if delta:
                act = payload[pl.ds(example * TOK, TOK), :]
            else:
                act = own_acts[example]
            grad = jnp.dot(grads[example], act, preferred_element_type=jnp.float32)
            signed = grad * signs[delta]
            parts = []
            for b in range(4):
                both = jnp.concatenate(split(signed[b * COLS : (b + 1) * COLS]), axis=0)
                parts.append(jnp.dot(had, both, preferred_element_type=jnp.float32))
            p0_, p1_ = parts[0] + parts[1], parts[0] - parts[1]
            p2_, p3_ = parts[2] + parts[3], parts[2] - parts[3]
            for a, value in enumerate((p0_ + p2_, p1_ + p3_, p0_ - p2_, p1_ - p3_)):
                value = value.astype(jnp.bfloat16)
                for i in range(4):
                    tiles[4 * a + i, example, block] = value[i * LOW : (i + 1) * LOW]

    def tile_body(tile, carry):
        idx = jnp.concatenate([idx_ref[pl.ds(tx * NZ + tile, 1), :] for tx in range(NX)], axis=1)
        line = lax.broadcasted_iota(jnp.int32, (16, SAMPLES), 0)
        low_signs = sign_of(line & idx)
        high_signs = sign_of(line & (idx >> 4))
        weights = jnp.concatenate(
            [(low_signs * high_signs[a : a + 1]).astype(jnp.bfloat16) for a in range(16)], axis=0
        )
        sign_xz = sign_of(((idx >> 8) & 15 & z) | (((idx >> 24) & 3 & x) << 4))
        sign_1 = sign_of((idx >> 12) & 1)
        sign_2 = sign_of((idx >> 13) & 1)
        chosen = lax.broadcasted_iota(jnp.int32, (LOW, SAMPLES), 0) == ((idx >> 14) & (LOW - 1))
        left = tiles[tile].reshape(2 * NX * LOW, COLS)
        both = jnp.dot(left, weights, preferred_element_type=jnp.float32)
        for example in range(2):
            b0, b1, b2, b3 = [
                both[(example * NX + j) * LOW : (example * NX + j + 1) * LOW] for j in range(NX)
            ]
            total = (b0 + b1 * sign_1) + (b2 + b3 * sign_1) * sign_2
            picked = jnp.sum(jnp.where(chosen, total, 0.0), axis=0, keepdims=True) * sign_xz
            for tx in range(NX):
                out_ref[tx, tile & 3, tile >> 2, pl.ds(example, 1), :] = picked[:, tx * KDEV : (tx + 1) * KDEV]
        return carry

    lax.fori_loop(0, TILES, tile_body, 0, unroll=4)


def shards(activations, out_grads, sign_words, indices):
    ex = ("y", "core")
    ex_size = lax.axis_size(ex)
    vmem = pl.BlockSpec(memory_space=pltpu.VMEM)
    own_bytes, *payloads = pl.pallas_call(
        pack_kernel,
        out_shape=[jax.ShapeDtypeStruct((128, COLS), jnp.bfloat16)]
        + [jax.ShapeDtypeStruct((2 * TOK + 128, COLS), jnp.bfloat16)] * 3,
        in_specs=[vmem] * 2,
        out_specs=[vmem] * 4,
        compiler_params=pltpu.CompilerParams(vmem_limit_bytes=16 * 1024 * 1024),
        name="pack_columns_and_words",
    )(activations, jnp.transpose(sign_words, (1, 0)))
    payloads = [
        lax.ppermute(payload, "x", [(i, i ^ delta) for i in range(NX)])
        for delta, payload in enumerate(payloads, 1)
    ]

    wire = jnp.transpose(out_grads, (0, 2, 1)).astype(jnp.float32) * WIRE
    wire = lax.all_gather(wire.astype(jnp.float16), Z, axis=1, tiled=True)
    grads = wire.astype(jnp.float32).astype(jnp.bfloat16)

    values = pl.pallas_call(
        main_kernel,
        out_shape=jax.ShapeDtypeStruct((NX, 4, 4, 2, KDEV), jnp.float32),
        in_specs=[vmem] * 7,
        out_specs=vmem,
        scratch_shapes=[
            pltpu.VMEM((NX, ROWS, COLS), jnp.float32),
            pltpu.VMEM((TILES, 2, NX, LOW, COLS), jnp.bfloat16),
        ],
        compiler_params=pltpu.CompilerParams(vmem_limit_bytes=VMEM_BYTES),
        cost_estimate=pl.CostEstimate(
            flops=7 * 10**9, bytes_accessed=8 * 1024 * 1024, transcendentals=0
        ),
        name="gradient_transform_sample",
    )(indices.reshape(NX * NZ, KDEV), grads, own_bytes, activations, *payloads)

    near = lax.all_to_all(
        values.reshape(16, 4, 2, KDEV), ("x", "zl"), split_axis=0, concat_axis=0, tiled=True
    )
    half = jnp.sum(near, axis=0) * SCALE
    sent = jnp.broadcast_to(half[None], (ex_size, 4, 2, KDEV)).reshape(ex_size * 4, 2, KDEV)
    received = lax.all_to_all(sent, ex + ("zh",), split_axis=0, concat_axis=0, tiled=True)
    raw = jnp.sum(received.reshape(ex_size, 4, 2, KDEV), axis=1)
    own_raw = lax.dynamic_index_in_dim(raw, lax.axis_index(ex), axis=0, keepdims=False)
    return own_raw - jnp.sum(raw, axis=(0, 1))[None, :] / (2 * ex_size)


def solution(mesh):
    grid = Mesh(mesh.devices.reshape(-1, 2, NX, 4, 4), ("y", "core", "x") + Z)
    ex, par = ("y", "core"), ("x",) + Z
    return jax.shard_map(
        shards,
        mesh=grid,
        in_specs=(P(ex, None, par), P(ex, None, par), P(None, par), P()),
        out_specs=P(ex, par),
        check_vma=False,
    )
```

```python
import jax
import jax.numpy as jnp
from jax import lax
from jax.experimental import pallas as pl
from jax.experimental.pallas import tpu as pltpu
from jax.sharding import Mesh, PartitionSpec as P

D = 4096
FF = 16384
TOK = 512
NX = 4
NZ = 16
ROWS = D // NX
COLS = 256
LOW = 64
TILES = ROWS // LOW
KDEV = 128
SAMPLES = NX * KDEV
WIRE = 131072.0
SCALE = 1.0 / 8192.0 / WIRE
VMEM_BYTES = 36 * 1024 * 1024


def sign_of(bits):
    bits = bits ^ (bits >> 4)
    bits = bits ^ (bits >> 2)
    bits = bits ^ (bits >> 1)
    return (1 - 2 * (bits & 1)).astype(jnp.float32)


def split(values):
    high = values.astype(jnp.bfloat16)
    return high, (values - high.astype(jnp.float32)).astype(jnp.bfloat16)


def pack_kernel(acts_in, words_in, *refs):
    payloads, (words, packed, word_sem, act_sem, out_sem) = refs[:NX], refs[NX:]
    x = lax.axis_index("x")
    copies = []
    for delta in range(NX):
        start = pl.multiple_of((x ^ delta) * ROWS, ROWS)
        source = words_in.at[:, pl.ds(start, ROWS)]
        copies.append(pltpu.make_async_copy(source, words.at[delta], word_sem.at[delta]))
    for delta in range(NX):
        for example in range(2):
            target = payloads[delta].at[pl.ds(example * TOK, TOK)]
            sem = act_sem.at[delta, example]
            copies.append(pltpu.make_async_copy(acts_in.at[example], target, sem))
    for copy in copies:
        copy.start()
    for delta in range(NX):
        copies[delta].wait()
        word = words[delta]
        two = jnp.concatenate([word & 255, (word >> 8) & 255], axis=0)
        two = two.astype(jnp.float32).astype(jnp.bfloat16)
        for q in range(4):
            packed[delta, pl.ds(32 * q, 32), :] = two[:, q * COLS : (q + 1) * COLS]
        target = payloads[delta].at[pl.ds(2 * TOK, 128)]
        copies.append(pltpu.make_async_copy(packed.at[delta], target, out_sem.at[delta]))
        copies[-1].start()
    for copy in copies[NX:]:
        copy.wait()


def main_kernel(idx_ref, grads, p0, p1, p2, p3, out_ref, signs, tiles):
    x, z = lax.axis_index("x"), lax.axis_index("z")

    row = lax.broadcasted_iota(jnp.int32, (COLS, COLS), 0)
    col = lax.broadcasted_iota(jnp.int32, (COLS, COLS), 1)
    had = sign_of(row & col).astype(jnp.bfloat16)
    had = jnp.concatenate([had, had], axis=1)
    byte_row = lax.broadcasted_iota(jnp.int32, (32, COLS), 0)
    byte_col = lax.broadcasted_iota(jnp.int32, (32, COLS), 1)
    spread = (byte_row == (byte_col >> 4) + 16 * ((byte_col >> 3) & 1)).astype(jnp.float32)
    spread = spread.astype(jnp.bfloat16)
    shift = lax.broadcasted_iota(jnp.int32, (COLS, COLS), 1) & 7

    for delta, payload in enumerate((p0, p1, p2, p3)):
        block = x ^ delta
        for q in range(4):
            two = payload[pl.ds(2 * TOK + 32 * q, 32), :]
            value = lax.dot_general(
                two, spread, (((0,), (0,)), ((), ())), preferred_element_type=jnp.float32
            )
            bit = (value.astype(jnp.int32) >> shift) & 1
            signs[delta, pl.ds(q * COLS, COLS), :] = (1 - 2 * bit).astype(jnp.float32)
        for example in range(2):
            act = payload[pl.ds(example * TOK, TOK), :]
            grad = jnp.dot(grads[example], act, preferred_element_type=jnp.float32)
            signed = grad * signs[delta]
            parts = []
            for b in range(4):
                both = jnp.concatenate(split(signed[b * COLS : (b + 1) * COLS]), axis=0)
                parts.append(jnp.dot(had, both, preferred_element_type=jnp.float32))
            p0_, p1_ = parts[0] + parts[1], parts[0] - parts[1]
            p2_, p3_ = parts[2] + parts[3], parts[2] - parts[3]
            for a, value in enumerate((p0_ + p2_, p1_ + p3_, p0_ - p2_, p1_ - p3_)):
                value = value.astype(jnp.bfloat16)
                for i in range(4):
                    tiles[4 * a + i, example, block] = value[i * LOW : (i + 1) * LOW]

    def tile_body(tile, carry):
        idx = jnp.concatenate([idx_ref[pl.ds(tx * NZ + tile, 1), :] for tx in range(NX)], axis=1)
        line = lax.broadcasted_iota(jnp.int32, (16, SAMPLES), 0)
        low_signs = sign_of(line & idx)
        high_signs = sign_of(line & (idx >> 4))
        weights = jnp.concatenate(
            [(low_signs * high_signs[a : a + 1]).astype(jnp.bfloat16) for a in range(16)], axis=0
        )
        sign_xz = sign_of(((idx >> 8) & 15 & z) | (((idx >> 24) & 3 & x) << 4))
        sign_1 = sign_of((idx >> 12) & 1)
        sign_2 = sign_of((idx >> 13) & 1)
        chosen = lax.broadcasted_iota(jnp.int32, (LOW, SAMPLES), 0) == ((idx >> 14) & (LOW - 1))
        left = tiles[tile].reshape(2 * NX * LOW, COLS)
        both = jnp.dot(left, weights, preferred_element_type=jnp.float32)
        for example in range(2):
            b0, b1, b2, b3 = [
                both[(example * NX + j) * LOW : (example * NX + j + 1) * LOW] for j in range(NX)
            ]
            total = (b0 + b1 * sign_1) + (b2 + b3 * sign_1) * sign_2
            picked = jnp.sum(jnp.where(chosen, total, 0.0), axis=0, keepdims=True) * sign_xz
            for tx in range(NX):
                out_ref[tile, tx, pl.ds(example, 1), :] = picked[:, tx * KDEV : (tx + 1) * KDEV]
        return carry

    lax.fori_loop(0, TILES, tile_body, 0, unroll=4)


def shards(activations, out_grads, sign_words, indices):
    ex = ("y", "core")
    ex_size = lax.axis_size(ex)
    vmem = pl.BlockSpec(memory_space=pltpu.VMEM)
    hbm = pl.BlockSpec(memory_space=pltpu.HBM)
    payloads = pl.pallas_call(
        pack_kernel,
        out_shape=[jax.ShapeDtypeStruct((2 * TOK + 128, COLS), jnp.bfloat16)] * NX,
        in_specs=[hbm] * 2,
        out_specs=[hbm] * NX,
        scratch_shapes=[
            pltpu.VMEM((NX, FF // 1024, ROWS), jnp.int32),
            pltpu.VMEM((NX, 128, COLS), jnp.bfloat16),
            pltpu.SemaphoreType.DMA((NX,)),
            pltpu.SemaphoreType.DMA((NX, 2)),
            pltpu.SemaphoreType.DMA((NX,)),
        ],
        compiler_params=pltpu.CompilerParams(vmem_limit_bytes=60 * 1024 * 1024),
        name="pack_columns_and_words",
    )(activations, jnp.transpose(sign_words, (1, 0)))
    payloads = [
        lax.ppermute(payload, "x", [(i, i ^ delta) for i in range(NX)]) if delta else payload
        for delta, payload in enumerate(payloads)
    ]

    wire = jnp.transpose(out_grads, (0, 2, 1)).astype(jnp.float32) * WIRE
    wire = lax.all_gather(wire.astype(jnp.float16), ("z", "core"), axis=1, tiled=True)
    wire = lax.dynamic_index_in_dim(
        wire.reshape(2, NZ, 2, LOW, TOK), lax.axis_index("core"), axis=2, keepdims=False
    )
    grads = wire.reshape(2, ROWS, TOK).astype(jnp.float32).astype(jnp.bfloat16)

    values = pl.pallas_call(
        main_kernel,
        out_shape=jax.ShapeDtypeStruct((TILES, NX, 2, KDEV), jnp.float32),
        in_specs=[vmem] * 6,
        out_specs=vmem,
        scratch_shapes=[
            pltpu.VMEM((NX, ROWS, COLS), jnp.float32),
            pltpu.VMEM((TILES, 2, NX, LOW, COLS), jnp.bfloat16),
        ],
        compiler_params=pltpu.CompilerParams(vmem_limit_bytes=VMEM_BYTES),
        cost_estimate=pl.CostEstimate(
            flops=7 * 10**9, bytes_accessed=8 * 1024 * 1024, transcendentals=0
        ),
        name="gradient_transform_sample",
    )(indices.reshape(NX * NZ, KDEV), grads, *payloads)

    along_z = lax.all_to_all(values, "z", split_axis=0, concat_axis=0, tiled=True)
    half = jnp.sum(along_z, axis=0) * SCALE
    sent = jnp.broadcast_to(half[None], (ex_size, NX, 2, KDEV)).reshape(ex_size * NX, 2, KDEV)
    received = lax.all_to_all(sent, ex + ("x",), split_axis=0, concat_axis=0, tiled=True)
    raw = jnp.sum(received.reshape(ex_size, NX, 2, KDEV), axis=1)
    own_raw = lax.dynamic_index_in_dim(raw, lax.axis_index(ex), axis=0, keepdims=False)
    return own_raw - jnp.sum(raw, axis=(0, 1))[None, :] / (2 * ex_size)


def solution(mesh):
    grid = Mesh(mesh.devices.reshape(-1, 2, NX, NZ), ("y", "core", "x", "z"))
    ex, par = ("y", "core"), ("x", "z")
    return jax.shard_map(
        shards,
        mesh=grid,
        in_specs=(P(ex, None, par), P(ex, None, par), P(None, par), P()),
        out_specs=P(ex, par),
        check_vma=False,
    )
```

```python
import jax
import jax.numpy as jnp
from jax import lax
from jax.experimental import pallas as pl
from jax.experimental.pallas import tpu as pltpu
from jax.sharding import Mesh, PartitionSpec as P

D = 4096
FF = 16384
TOK = 512
NX = 4
NZ = 16
ROWS = D // NX
COLS = 256
LOW = 64
TILES = ROWS // LOW
KDEV = 128
SAMPLES = NX * KDEV
WIRE = 131072.0
SCALE = 1.0 / 8192.0 / WIRE
VMEM_BYTES = 36 * 1024 * 1024


def sign_of(bits):
    bits = bits ^ (bits >> 4)
    bits = bits ^ (bits >> 2)
    bits = bits ^ (bits >> 1)
    return (1 - 2 * (bits & 1)).astype(jnp.float32)


def split(values):
    high = values.astype(jnp.bfloat16)
    return high, (values - high.astype(jnp.float32)).astype(jnp.bfloat16)


def pack_kernel(acts_ref, words_ref, out_ref):
    for target in range(NX):
        for example in range(2):
            out_ref[target, pl.ds(example * TOK, TOK), :] = acts_ref[example]
        word = words_ref[:, target * ROWS : (target + 1) * ROWS]
        two = jnp.concatenate([word & 255, (word >> 8) & 255], axis=0)
        two = two.astype(jnp.float32).astype(jnp.bfloat16)
        for q in range(4):
            part = two[:, q * COLS : (q + 1) * COLS]
            out_ref[target, pl.ds(2 * TOK + 32 * q, 32), :] = part


def main_kernel(idx_ref, grads, columns, out_ref, signs, tiles):
    x, z = lax.axis_index("x"), lax.axis_index("z")

    row = lax.broadcasted_iota(jnp.int32, (COLS, COLS), 0)
    col = lax.broadcasted_iota(jnp.int32, (COLS, COLS), 1)
    had = sign_of(row & col).astype(jnp.bfloat16)
    had = jnp.concatenate([had, had], axis=1)
    byte_row = lax.broadcasted_iota(jnp.int32, (32, COLS), 0)
    byte_col = lax.broadcasted_iota(jnp.int32, (32, COLS), 1)
    spread = (byte_row == (byte_col >> 4) + 16 * ((byte_col >> 3) & 1)).astype(jnp.float32)
    spread = spread.astype(jnp.bfloat16)
    shift = lax.broadcasted_iota(jnp.int32, (COLS, COLS), 1) & 7

    for block in range(NX):
        for q in range(4):
            two = columns[block, pl.ds(2 * TOK + 32 * q, 32), :]
            value = lax.dot_general(
                two, spread, (((0,), (0,)), ((), ())), preferred_element_type=jnp.float32
            )
            bit = (value.astype(jnp.int32) >> shift) & 1
            signs[block, pl.ds(q * COLS, COLS), :] = (1 - 2 * bit).astype(jnp.float32)
        for example in range(2):
            act = columns[block, pl.ds(example * TOK, TOK), :]
            grad = jnp.dot(grads[example], act, preferred_element_type=jnp.float32)
            signed = grad * signs[block]
            parts = []
            for b in range(4):
                both = jnp.concatenate(split(signed[b * COLS : (b + 1) * COLS]), axis=0)
                parts.append(jnp.dot(had, both, preferred_element_type=jnp.float32))
            p0_, p1_ = parts[0] + parts[1], parts[0] - parts[1]
            p2_, p3_ = parts[2] + parts[3], parts[2] - parts[3]
            for a, value in enumerate((p0_ + p2_, p1_ + p3_, p0_ - p2_, p1_ - p3_)):
                value = value.astype(jnp.bfloat16)
                for i in range(4):
                    tiles[4 * a + i, example, block] = value[i * LOW : (i + 1) * LOW]

    def tile_body(tile, carry):
        idx = jnp.concatenate([idx_ref[pl.ds(tx * NZ + tile, 1), :] for tx in range(NX)], axis=1)
        line = lax.broadcasted_iota(jnp.int32, (16, SAMPLES), 0)
        low_signs = sign_of(line & idx)
        high_signs = sign_of(line & (idx >> 4))
        weights = jnp.concatenate(
            [(low_signs * high_signs[a : a + 1]).astype(jnp.bfloat16) for a in range(16)], axis=0
        )
        sign_xz = sign_of(((idx >> 8) & 15 & z) | (((idx >> 24) & 3 & x) << 4))
        sign_1 = sign_of((idx >> 12) & 1)
        sign_2 = sign_of((idx >> 13) & 1)
        chosen = lax.broadcasted_iota(jnp.int32, (LOW, SAMPLES), 0) == ((idx >> 14) & (LOW - 1))
        left = tiles[tile].reshape(2 * NX * LOW, COLS)
        both = jnp.dot(left, weights, preferred_element_type=jnp.float32)
        for example in range(2):
            b0, b1, b2, b3 = [
                both[(example * NX + j) * LOW : (example * NX + j + 1) * LOW] for j in range(NX)
            ]
            total = (b0 + b1 * sign_1) + (b2 + b3 * sign_1) * sign_2
            picked = jnp.sum(jnp.where(chosen, total, 0.0), axis=0, keepdims=True) * sign_xz
            for tx in range(NX):
                out_ref[tile, tx, pl.ds(example, 1), :] = picked[:, tx * KDEV : (tx + 1) * KDEV]
        return carry

    lax.fori_loop(0, TILES, tile_body, 0, unroll=4)


def shards(activations, out_grads, sign_words, indices):
    ex = ("y", "core")
    ex_size = lax.axis_size(ex)
    vmem = pl.BlockSpec(memory_space=pltpu.VMEM)
    packed = pl.pallas_call(
        pack_kernel,
        out_shape=jax.ShapeDtypeStruct((NX, 2 * TOK + 128, COLS), jnp.bfloat16),
        in_specs=[vmem] * 2,
        out_specs=vmem,
        compiler_params=pltpu.CompilerParams(vmem_limit_bytes=16 * 1024 * 1024),
        name="pack_columns_and_words",
    )(activations, jnp.transpose(sign_words, (1, 0)))
    columns = lax.all_to_all(packed, "x", split_axis=0, concat_axis=0, tiled=True)

    wire = jnp.transpose(out_grads, (0, 2, 1)).astype(jnp.float32) * WIRE
    wire = lax.all_gather(wire.astype(jnp.float16), "z", axis=1, tiled=True)
    grads = wire.astype(jnp.float32).astype(jnp.bfloat16)

    values = pl.pallas_call(
        main_kernel,
        out_shape=jax.ShapeDtypeStruct((TILES, NX, 2, KDEV), jnp.float32),
        in_specs=[vmem] * 3,
        out_specs=vmem,
        scratch_shapes=[
            pltpu.VMEM((NX, ROWS, COLS), jnp.float32),
            pltpu.VMEM((TILES, 2, NX, LOW, COLS), jnp.bfloat16),
        ],
        compiler_params=pltpu.CompilerParams(vmem_limit_bytes=VMEM_BYTES),
        cost_estimate=pl.CostEstimate(
            flops=7 * 10**9, bytes_accessed=8 * 1024 * 1024, transcendentals=0
        ),
        name="gradient_transform_sample",
    )(indices.reshape(NX * NZ, KDEV), grads, columns)

    along_z = lax.all_to_all(values, "z", split_axis=0, concat_axis=0, tiled=True)
    half = jnp.sum(along_z, axis=0) * SCALE
    sent = jnp.broadcast_to(half[None], (ex_size, NX, 2, KDEV)).reshape(ex_size * NX, 2, KDEV)
    received = lax.all_to_all(sent, ex + ("x",), split_axis=0, concat_axis=0, tiled=True)
    raw = jnp.sum(received.reshape(ex_size, NX, 2, KDEV), axis=1)
    own_raw = lax.dynamic_index_in_dim(raw, lax.axis_index(ex), axis=0, keepdims=False)
    return own_raw - jnp.sum(raw, axis=(0, 1))[None, :] / (2 * ex_size)


def solution(mesh):
    grid = Mesh(mesh.devices.reshape(-1, 2, NX, NZ), ("y", "core", "x", "z"))
    ex, par = ("y", "core"), ("x", "z")
    return jax.shard_map(
        shards,
        mesh=grid,
        in_specs=(P(ex, None, par), P(ex, None, par), P(None, par), P()),
        out_specs=P(ex, par),
        check_vma=False,
    )
```

```python
import jax
import jax.numpy as jnp
from jax import lax
from jax.experimental import pallas as pl
from jax.experimental.pallas import tpu as pltpu
from jax.sharding import Mesh, PartitionSpec as P

D = 4096
FF = 16384
TOK = 512
NX = 4
NZ = 16
ROWS = D // NX
COLS = 256
LOW = 64
TILES = ROWS // LOW
KDEV = 128
SAMPLES = NX * KDEV
WIRE = 131072.0
SCALE = 1.0 / 8192.0 / WIRE
VMEM_BYTES = 20 * 1024 * 1024


def sign_of(bits):
    bits = bits ^ (bits >> 4)
    bits = bits ^ (bits >> 2)
    bits = bits ^ (bits >> 1)
    return (1 - 2 * (bits & 1)).astype(jnp.float32)


def split(values):
    high = values.astype(jnp.bfloat16)
    return high, (values - high.astype(jnp.float32)).astype(jnp.bfloat16)


def pack_kernel(acts_in, words_in, out, acts, words, packed, in_sem, act_sem, byte_sem):
    word_copy = pltpu.make_async_copy(words_in, words, in_sem.at[2])
    word_copy.start()
    act_copies = []
    for example in range(2):
        target = acts.at[pl.ds(example * TOK, TOK)]
        act_copies.append(pltpu.make_async_copy(acts_in.at[example], target, in_sem.at[example]))
        act_copies[-1].start()
    copies = []
    word_copy.wait()
    for target in range(NX):
        word = words[:, target * ROWS : (target + 1) * ROWS]
        two = jnp.concatenate([word & 255, (word >> 8) & 255], axis=0)
        two = two.astype(jnp.float32).astype(jnp.bfloat16)
        for q in range(4):
            packed[target, pl.ds(32 * q, 32), :] = two[:, q * COLS : (q + 1) * COLS]
    for copy in act_copies:
        copy.wait()
    for target in range(NX):
        head, tail = out.at[target, pl.ds(0, 2 * TOK)], out.at[target, pl.ds(2 * TOK, 128)]
        copies.append(pltpu.make_async_copy(acts, head, act_sem.at[target]))
        copies.append(pltpu.make_async_copy(packed.at[target], tail, byte_sem.at[target]))
    for copy in copies:
        copy.start()
    for copy in copies:
        copy.wait()


def main_kernel(idx_ref, grads, columns, out_ref, signs, tiles):
    x, z = lax.axis_index("x"), lax.axis_index("z")

    row = lax.broadcasted_iota(jnp.int32, (COLS, COLS), 0)
    col = lax.broadcasted_iota(jnp.int32, (COLS, COLS), 1)
    had = sign_of(row & col).astype(jnp.bfloat16)
    had = jnp.concatenate([had, had], axis=1)
    byte_row = lax.broadcasted_iota(jnp.int32, (32, COLS), 0)
    byte_col = lax.broadcasted_iota(jnp.int32, (32, COLS), 1)
    spread = (byte_row == (byte_col >> 4) + 16 * ((byte_col >> 3) & 1)).astype(jnp.float32)
    spread = spread.astype(jnp.bfloat16)
    shift = lax.broadcasted_iota(jnp.int32, (COLS, COLS), 1) & 7

    for block in range(NX):
        for q in range(4):
            two = columns[block, pl.ds(2 * TOK + 32 * q, 32), :]
            value = lax.dot_general(
                two, spread, (((0,), (0,)), ((), ())), preferred_element_type=jnp.float32
            )
            bit = (value.astype(jnp.int32) >> shift) & 1
            signs[block, pl.ds(q * COLS, COLS), :] = (1 - 2 * bit).astype(jnp.float32)
        for example in range(2):
            act = columns[block, pl.ds(example * TOK, TOK), :]
            grad = jnp.dot(grads[example], act, preferred_element_type=jnp.float32)
            signed = grad * signs[block]
            parts = []
            for b in range(4):
                both = jnp.concatenate(split(signed[b * COLS : (b + 1) * COLS]), axis=0)
                parts.append(jnp.dot(had, both, preferred_element_type=jnp.float32))
            p0_, p1_ = parts[0] + parts[1], parts[0] - parts[1]
            p2_, p3_ = parts[2] + parts[3], parts[2] - parts[3]
            for a, value in enumerate((p0_ + p2_, p1_ + p3_, p0_ - p2_, p1_ - p3_)):
                value = value.astype(jnp.bfloat16)
                for i in range(4):
                    tiles[4 * a + i, example, block] = value[i * LOW : (i + 1) * LOW]

    def tile_body(tile, carry):
        idx = jnp.concatenate([idx_ref[pl.ds(tx * NZ + tile, 1), :] for tx in range(NX)], axis=1)
        line = lax.broadcasted_iota(jnp.int32, (16, SAMPLES), 0)
        low_signs = sign_of(line & idx)
        high_signs = sign_of(line & (idx >> 4))
        weights = jnp.concatenate(
            [(low_signs * high_signs[a : a + 1]).astype(jnp.bfloat16) for a in range(16)], axis=0
        )
        sign_xz = sign_of(((idx >> 8) & 15 & z) | (((idx >> 24) & 3 & x) << 4))
        sign_1 = sign_of((idx >> 12) & 1)
        sign_2 = sign_of((idx >> 13) & 1)
        chosen = lax.broadcasted_iota(jnp.int32, (LOW, SAMPLES), 0) == ((idx >> 14) & (LOW - 1))
        left = tiles[tile].reshape(2 * NX * LOW, COLS)
        both = jnp.dot(left, weights, preferred_element_type=jnp.float32)
        for example in range(2):
            b0, b1, b2, b3 = [
                both[(example * NX + j) * LOW : (example * NX + j + 1) * LOW] for j in range(NX)
            ]
            total = (b0 + b1 * sign_1) + (b2 + b3 * sign_1) * sign_2
            picked = jnp.sum(jnp.where(chosen, total, 0.0), axis=0, keepdims=True) * sign_xz
            for tx in range(NX):
                out_ref[tile, tx, pl.ds(example, 1), :] = picked[:, tx * KDEV : (tx + 1) * KDEV]
        return carry

    lax.fori_loop(0, TILES, tile_body, 0, unroll=8)


def shards(activations, out_grads, sign_words, indices):
    ex = ("y", "core")
    ex_size = lax.axis_size(ex)
    vmem = pl.BlockSpec(memory_space=pltpu.VMEM)
    hbm = pl.BlockSpec(memory_space=pltpu.HBM)
    packed = pl.pallas_call(
        pack_kernel,
        out_shape=jax.ShapeDtypeStruct((NX, 2 * TOK + 128, COLS), jnp.bfloat16),
        in_specs=[hbm] * 2,
        out_specs=hbm,
        scratch_shapes=[
            pltpu.VMEM((2 * TOK, COLS), jnp.bfloat16),
            pltpu.VMEM((FF // 1024, D), jnp.int32),
            pltpu.VMEM((NX, 128, COLS), jnp.bfloat16),
            pltpu.SemaphoreType.DMA((3,)),
            pltpu.SemaphoreType.DMA((NX,)),
            pltpu.SemaphoreType.DMA((NX,)),
        ],
        compiler_params=pltpu.CompilerParams(vmem_limit_bytes=60 * 1024 * 1024),
        name="pack_columns_and_words",
    )(activations, jnp.transpose(sign_words, (1, 0)))
    columns = lax.all_to_all(packed, "x", split_axis=0, concat_axis=0, tiled=True)

    wire = jnp.transpose(out_grads, (0, 2, 1)).astype(jnp.float32) * WIRE
    wire = lax.all_gather(wire.astype(jnp.float16), "z", axis=1, tiled=True)
    grads = wire.astype(jnp.float32).astype(jnp.bfloat16)

    values = pl.pallas_call(
        main_kernel,
        out_shape=jax.ShapeDtypeStruct((TILES, NX, 2, KDEV), jnp.float32),
        in_specs=[vmem] * 3,
        out_specs=vmem,
        scratch_shapes=[
            pltpu.VMEM((NX, ROWS, COLS), jnp.float32),
            pltpu.VMEM((TILES, 2, NX, LOW, COLS), jnp.bfloat16),
        ],
        compiler_params=pltpu.CompilerParams(
            vmem_limit_bytes=VMEM_BYTES, allow_input_fusion=[False, True, False]
        ),
        cost_estimate=pl.CostEstimate(
            flops=7 * 10**9, bytes_accessed=8 * 1024 * 1024, transcendentals=0
        ),
        name="gradient_transform_sample",
    )(indices.reshape(NX * NZ, KDEV), grads, columns)

    along_z = lax.all_to_all(values, "z", split_axis=0, concat_axis=0, tiled=True)
    half = jnp.sum(along_z, axis=0) * SCALE
    sent = jnp.broadcast_to(half[None], (ex_size, NX, 2, KDEV)).reshape(ex_size * NX, 2, KDEV)
    received = lax.all_to_all(sent, ex + ("x",), split_axis=0, concat_axis=0, tiled=True)
    raw = jnp.sum(received.reshape(ex_size, NX, 2, KDEV), axis=1)
    own_raw = lax.dynamic_index_in_dim(raw, lax.axis_index(ex), axis=0, keepdims=False)
    return own_raw - jnp.sum(raw, axis=(0, 1))[None, :] / (2 * ex_size)


def solution(mesh):
    grid = Mesh(mesh.devices.reshape(-1, 2, NX, NZ), ("y", "core", "x", "z"))
    ex, par = ("y", "core"), ("x", "z")
    return jax.shard_map(
        shards,
        mesh=grid,
        in_specs=(P(ex, None, par), P(ex, None, par), P(None, par), P()),
        out_specs=P(ex, par),
        check_vma=False,
    )
```

```python
import jax
import jax.numpy as jnp
from jax import lax
from jax.experimental import pallas as pl
from jax.experimental.pallas import tpu as pltpu
from jax.sharding import Mesh, PartitionSpec as P

D = 4096
FF = 16384
TOK = 512
NX = 4
NZ = 16
ROWS = D // NX
COLS = 256
LOW = 64
TILES = ROWS // LOW
KDEV = 128
SAMPLES = NX * KDEV
WIRE = 131072.0
SCALE = 1.0 / 8192.0 / WIRE
VMEM_BYTES = 20 * 1024 * 1024


def sign_of(bits):
    bits = bits ^ (bits >> 4)
    bits = bits ^ (bits >> 2)
    bits = bits ^ (bits >> 1)
    return (1 - 2 * (bits & 1)).astype(jnp.float32)


def split(values):
    high = values.astype(jnp.bfloat16)
    return high, (values - high.astype(jnp.float32)).astype(jnp.bfloat16)


def pack_kernel(acts_in, words_in, out, acts, words, packed, in_sem, act_sem, byte_sem):
    word_copy = pltpu.make_async_copy(words_in, words, in_sem.at[2])
    word_copy.start()
    act_copies = []
    for example in range(2):
        target = acts.at[pl.ds(example * TOK, TOK)]
        act_copies.append(pltpu.make_async_copy(acts_in.at[example], target, in_sem.at[example]))
        act_copies[-1].start()
    copies = []
    word_copy.wait()
    for target in range(NX):
        word = words[:, target * ROWS : (target + 1) * ROWS]
        two = jnp.concatenate([word & 255, (word >> 8) & 255], axis=0)
        two = two.astype(jnp.float32).astype(jnp.bfloat16)
        for q in range(4):
            packed[target, pl.ds(32 * q, 32), :] = two[:, q * COLS : (q + 1) * COLS]
    for copy in act_copies:
        copy.wait()
    for target in range(NX):
        head, tail = out.at[target, pl.ds(0, 2 * TOK)], out.at[target, pl.ds(2 * TOK, 128)]
        copies.append(pltpu.make_async_copy(acts, head, act_sem.at[target]))
        copies.append(pltpu.make_async_copy(packed.at[target], tail, byte_sem.at[target]))
    for copy in copies:
        copy.start()
    for copy in copies:
        copy.wait()


def main_kernel(idx_ref, grads, columns, out_ref, signs, tiles):
    x, z = lax.axis_index("x"), lax.axis_index("z")

    row = lax.broadcasted_iota(jnp.int32, (COLS, COLS), 0)
    col = lax.broadcasted_iota(jnp.int32, (COLS, COLS), 1)
    had = sign_of(row & col).astype(jnp.bfloat16)
    had = jnp.concatenate([had, had], axis=1)
    byte_row = lax.broadcasted_iota(jnp.int32, (32, COLS), 0)
    byte_col = lax.broadcasted_iota(jnp.int32, (32, COLS), 1)
    chosen_byte = byte_row == (byte_col >> 4) + 16 * ((byte_col >> 3) & 1)
    spread = jnp.where(chosen_byte, 128 >> (byte_col & 7), 0).astype(jnp.float32)
    spread = spread.astype(jnp.bfloat16)

    for block in range(NX):
        for q in range(4):
            two = columns[block, pl.ds(2 * TOK + 32 * q, 32), :]
            value = lax.dot_general(
                two, spread, (((0,), (0,)), ((), ())), preferred_element_type=jnp.float32
            )
            bit = (value.astype(jnp.int32) & 128).astype(jnp.float32)
            signs[block, pl.ds(q * COLS, COLS), :] = 1.0 - bit * (1.0 / 64.0)
        for example in range(2):
            act = columns[block, pl.ds(example * TOK, TOK), :]
            grad = jnp.dot(grads[example], act, preferred_element_type=jnp.float32)
            signed = grad * signs[block]
            parts = []
            for b in range(4):
                both = jnp.concatenate(split(signed[b * COLS : (b + 1) * COLS]), axis=0)
                parts.append(jnp.dot(had, both, preferred_element_type=jnp.float32))
            p0_, p1_ = parts[0] + parts[1], parts[0] - parts[1]
            p2_, p3_ = parts[2] + parts[3], parts[2] - parts[3]
            for a, value in enumerate((p0_ + p2_, p1_ + p3_, p0_ - p2_, p1_ - p3_)):
                value = value.astype(jnp.bfloat16)
                for i in range(4):
                    tiles[4 * a + i, example, block] = value[i * LOW : (i + 1) * LOW]

    def tile_body(tile, carry):
        idx = jnp.concatenate([idx_ref[pl.ds(tx * NZ + tile, 1), :] for tx in range(NX)], axis=1)
        line = lax.broadcasted_iota(jnp.int32, (16, SAMPLES), 0)
        low_signs = sign_of(line & idx).astype(jnp.bfloat16)
        high_signs = sign_of(line & (idx >> 4)).astype(jnp.bfloat16)
        weights = jnp.concatenate(
            [low_signs * high_signs[a : a + 1] for a in range(16)], axis=0
        )
        sign_xz = sign_of(((idx >> 8) & 15 & z) | (((idx >> 24) & 3 & x) << 4))
        sign_1 = sign_of((idx >> 12) & 1)
        sign_2 = sign_of((idx >> 13) & 1)
        chosen = lax.broadcasted_iota(jnp.int32, (LOW, SAMPLES), 0) == ((idx >> 14) & (LOW - 1))
        left = tiles[tile].reshape(2 * NX * LOW, COLS)
        both = jnp.dot(left, weights, preferred_element_type=jnp.float32)
        for example in range(2):
            b0, b1, b2, b3 = [
                both[(example * NX + j) * LOW : (example * NX + j + 1) * LOW] for j in range(NX)
            ]
            total = (b0 + b1 * sign_1) + (b2 + b3 * sign_1) * sign_2
            picked = jnp.sum(jnp.where(chosen, total, 0.0), axis=0, keepdims=True) * sign_xz
            for tx in range(NX):
                out_ref[tile, tx, pl.ds(example, 1), :] = picked[:, tx * KDEV : (tx + 1) * KDEV]
        return carry

    lax.fori_loop(0, TILES, tile_body, 0, unroll=8)


def shards(activations, out_grads, sign_words, indices):
    ex = ("y", "core")
    ex_size = lax.axis_size(ex)
    vmem = pl.BlockSpec(memory_space=pltpu.VMEM)
    hbm = pl.BlockSpec(memory_space=pltpu.HBM)
    packed = pl.pallas_call(
        pack_kernel,
        out_shape=jax.ShapeDtypeStruct((NX, 2 * TOK + 128, COLS), jnp.bfloat16),
        in_specs=[hbm] * 2,
        out_specs=hbm,
        scratch_shapes=[
            pltpu.VMEM((2 * TOK, COLS), jnp.bfloat16),
            pltpu.VMEM((FF // 1024, D), jnp.int32),
            pltpu.VMEM((NX, 128, COLS), jnp.bfloat16),
            pltpu.SemaphoreType.DMA((3,)),
            pltpu.SemaphoreType.DMA((NX,)),
            pltpu.SemaphoreType.DMA((NX,)),
        ],
        compiler_params=pltpu.CompilerParams(vmem_limit_bytes=60 * 1024 * 1024),
        name="pack_columns_and_words",
    )(activations, jnp.transpose(sign_words, (1, 0)))
    columns = lax.all_to_all(packed, "x", split_axis=0, concat_axis=0, tiled=True)

    wire = jnp.transpose(out_grads, (0, 2, 1)).astype(jnp.float32) * WIRE
    wire = lax.all_gather(wire.astype(jnp.float16), "z", axis=1, tiled=True)
    wire, columns = lax.optimization_barrier((wire, columns))
    grads = wire.astype(jnp.float32).astype(jnp.bfloat16)

    values = pl.pallas_call(
        main_kernel,
        out_shape=jax.ShapeDtypeStruct((TILES, NX, 2, KDEV), jnp.float32),
        in_specs=[vmem] * 3,
        out_specs=vmem,
        scratch_shapes=[
            pltpu.VMEM((NX, ROWS, COLS), jnp.float32),
            pltpu.VMEM((TILES, 2, NX, LOW, COLS), jnp.bfloat16),
        ],
        compiler_params=pltpu.CompilerParams(
            vmem_limit_bytes=VMEM_BYTES, allow_input_fusion=[False, True, False]
        ),
        cost_estimate=pl.CostEstimate(
            flops=7 * 10**9, bytes_accessed=8 * 1024 * 1024, transcendentals=0
        ),
        name="gradient_transform_sample",
    )(indices.reshape(NX * NZ, KDEV), grads, columns)

    along_z = lax.all_to_all(values, "z", split_axis=0, concat_axis=0, tiled=True)
    half = jnp.sum(along_z, axis=0) * SCALE
    sent = jnp.broadcast_to(half[None], (ex_size, NX, 2, KDEV)).reshape(ex_size * NX, 2, KDEV)
    received = lax.all_to_all(sent, ex + ("x",), split_axis=0, concat_axis=0, tiled=True)
    raw = jnp.sum(received.reshape(ex_size, NX, 2, KDEV), axis=1)
    own_raw = lax.dynamic_index_in_dim(raw, lax.axis_index(ex), axis=0, keepdims=False)
    return own_raw - jnp.sum(raw, axis=(0, 1))[None, :] / (2 * ex_size)


def solution(mesh):
    grid = Mesh(mesh.devices.reshape(-1, 2, NX, NZ), ("y", "core", "x", "z"))
    ex, par = ("y", "core"), ("x", "z")
    return jax.shard_map(
        shards,
        mesh=grid,
        in_specs=(P(ex, None, par), P(ex, None, par), P(None, par), P()),
        out_specs=P(ex, par),
        check_vma=False,
    )
```

```python
import jax
import jax.numpy as jnp
from jax import lax
from jax.experimental import pallas as pl
from jax.experimental.pallas import tpu as pltpu
from jax.sharding import Mesh, PartitionSpec as P

D = 4096
FF = 16384
TOK = 512
NX = 4
NZ = 16
ROWS = D // NX
COLS = 256
LOW = 64
TILES = ROWS // LOW
KDEV = 128
SAMPLES = NX * KDEV
WIRE = 131072.0
SCALE = 1.0 / 8192.0 / WIRE
VMEM_BYTES = 20 * 1024 * 1024


def sign_of(bits):
    bits = bits ^ (bits >> 4)
    bits = bits ^ (bits >> 2)
    bits = bits ^ (bits >> 1)
    return (1 - 2 * (bits & 1)).astype(jnp.float32)


def split(values):
    high = values.astype(jnp.bfloat16)
    return high, (values - high.astype(jnp.float32)).astype(jnp.bfloat16)


def pack_kernel(acts_in, words_in, out, acts, words, packed, in_sem, act_sem, byte_sem):
    word_copy = pltpu.make_async_copy(words_in, words, in_sem.at[2])
    word_copy.start()
    act_copies = []
    for example in range(2):
        target = acts.at[pl.ds(example * TOK, TOK)]
        act_copies.append(pltpu.make_async_copy(acts_in.at[example], target, in_sem.at[example]))
        act_copies[-1].start()
    copies = []
    for copy in act_copies:
        copy.wait()
    for target in range(NX):
        head = out.at[target, pl.ds(0, 2 * TOK)]
        copies.append(pltpu.make_async_copy(acts, head, act_sem.at[target]))
        copies[-1].start()
    word_copy.wait()
    for target in range(NX):
        word = words[:, target * ROWS : (target + 1) * ROWS]
        two = jnp.concatenate([word & 255, (word >> 8) & 255], axis=0)
        two = two.astype(jnp.float32).astype(jnp.bfloat16)
        for q in range(4):
            packed[target, pl.ds(32 * q, 32), :] = two[:, q * COLS : (q + 1) * COLS]
        tail = out.at[target, pl.ds(2 * TOK, 128)]
        copies.append(pltpu.make_async_copy(packed.at[target], tail, byte_sem.at[target]))
        copies[-1].start()
    for copy in copies:
        copy.wait()


def main_kernel(idx_ref, grads_0, grads_1, columns, out_ref, signs, tiles):
    x, z = lax.axis_index("x"), lax.axis_index("z")

    row = lax.broadcasted_iota(jnp.int32, (COLS, COLS), 0)
    col = lax.broadcasted_iota(jnp.int32, (COLS, COLS), 1)
    had = sign_of(row & col).astype(jnp.bfloat16)
    had = jnp.concatenate([had, had], axis=1)
    byte_row = lax.broadcasted_iota(jnp.int32, (32, COLS), 0)
    byte_col = lax.broadcasted_iota(jnp.int32, (32, COLS), 1)
    chosen_byte = byte_row == (byte_col >> 4) + 16 * ((byte_col >> 3) & 1)
    spread = jnp.where(chosen_byte, 128 >> (byte_col & 7), 0).astype(jnp.float32)
    spread = spread.astype(jnp.bfloat16)

    for block in range(NX):
        for q in range(4):
            two = columns[block, pl.ds(2 * TOK + 32 * q, 32), :]
            value = lax.dot_general(
                two, spread, (((0,), (0,)), ((), ())), preferred_element_type=jnp.float32
            )
            bit = (value.astype(jnp.int32) & 128).astype(jnp.float32)
            signs[block, pl.ds(q * COLS, COLS), :] = 1.0 - bit * (1.0 / 64.0)
        for example, grads in enumerate((grads_0, grads_1)):
            act = columns[block, pl.ds(example * TOK, TOK), :]
            grad = jnp.dot(grads[...], act, preferred_element_type=jnp.float32)
            signed = grad * signs[block]
            parts = []
            for b in range(4):
                both = jnp.concatenate(split(signed[b * COLS : (b + 1) * COLS]), axis=0)
                parts.append(jnp.dot(had, both, preferred_element_type=jnp.float32))
            p0_, p1_ = parts[0] + parts[1], parts[0] - parts[1]
            p2_, p3_ = parts[2] + parts[3], parts[2] - parts[3]
            for a, value in enumerate((p0_ + p2_, p1_ + p3_, p0_ - p2_, p1_ - p3_)):
                value = value.astype(jnp.bfloat16)
                for i in range(4):
                    tiles[4 * a + i, example, block] = value[i * LOW : (i + 1) * LOW]

    def tile_body(tile, carry):
        idx = jnp.concatenate([idx_ref[pl.ds(tx * NZ + tile, 1), :] for tx in range(NX)], axis=1)
        line = lax.broadcasted_iota(jnp.int32, (16, SAMPLES), 0)
        low_signs = sign_of(line & idx).astype(jnp.bfloat16)
        high_signs = sign_of(line & (idx >> 4)).astype(jnp.bfloat16)
        weights = jnp.concatenate(
            [low_signs * high_signs[a : a + 1] for a in range(16)], axis=0
        )
        sign_xz = sign_of(((idx >> 8) & 15 & z) | (((idx >> 24) & 3 & x) << 4))
        sign_1 = sign_of((idx >> 12) & 1)
        sign_2 = sign_of((idx >> 13) & 1)
        chosen = lax.broadcasted_iota(jnp.int32, (LOW, SAMPLES), 0) == ((idx >> 14) & (LOW - 1))
        left = tiles[tile].reshape(2 * NX * LOW, COLS)
        both = jnp.dot(left, weights, preferred_element_type=jnp.float32)
        for example in range(2):
            b0, b1, b2, b3 = [
                both[(example * NX + j) * LOW : (example * NX + j + 1) * LOW] for j in range(NX)
            ]
            total = (b0 + b1 * sign_1) + (b2 + b3 * sign_1) * sign_2
            picked = jnp.sum(jnp.where(chosen, total, 0.0), axis=0, keepdims=True) * sign_xz
            for tx in range(NX):
                out_ref[tile, tx, pl.ds(example, 1), :] = picked[:, tx * KDEV : (tx + 1) * KDEV]
        return carry

    lax.fori_loop(0, TILES, tile_body, 0, unroll=8)


def shards(activations, out_grads, sign_words, indices):
    ex = ("y", "core")
    ex_size = lax.axis_size(ex)
    vmem = pl.BlockSpec(memory_space=pltpu.VMEM)
    hbm = pl.BlockSpec(memory_space=pltpu.HBM)
    packed = pl.pallas_call(
        pack_kernel,
        out_shape=jax.ShapeDtypeStruct((NX, 2 * TOK + 128, COLS), jnp.bfloat16),
        in_specs=[hbm] * 2,
        out_specs=hbm,
        scratch_shapes=[
            pltpu.VMEM((2 * TOK, COLS), jnp.bfloat16),
            pltpu.VMEM((FF // 1024, D), jnp.int32),
            pltpu.VMEM((NX, 128, COLS), jnp.bfloat16),
            pltpu.SemaphoreType.DMA((3,)),
            pltpu.SemaphoreType.DMA((NX,)),
            pltpu.SemaphoreType.DMA((NX,)),
        ],
        compiler_params=pltpu.CompilerParams(vmem_limit_bytes=60 * 1024 * 1024),
        name="pack_columns_and_words",
    )(activations, jnp.transpose(sign_words, (1, 0)))
    columns = lax.all_to_all(packed, "x", split_axis=0, concat_axis=0, tiled=True)

    wire = jnp.transpose(out_grads, (0, 2, 1)).astype(jnp.float32) * WIRE
    wire = lax.all_gather(wire.astype(jnp.float16), "z", axis=1, tiled=True)
    grads = [wire[example].astype(jnp.float32).astype(jnp.bfloat16) for example in range(2)]

    values = pl.pallas_call(
        main_kernel,
        out_shape=jax.ShapeDtypeStruct((TILES, NX, 2, KDEV), jnp.float32),
        in_specs=[vmem] * 4,
        out_specs=vmem,
        scratch_shapes=[
            pltpu.VMEM((NX, ROWS, COLS), jnp.float32),
            pltpu.VMEM((TILES, 2, NX, LOW, COLS), jnp.bfloat16),
        ],
        compiler_params=pltpu.CompilerParams(
            vmem_limit_bytes=VMEM_BYTES, allow_input_fusion=[False, True, True, False]
        ),
        cost_estimate=pl.CostEstimate(
            flops=7 * 10**9, bytes_accessed=8 * 1024 * 1024, transcendentals=0
        ),
        name="gradient_transform_sample",
    )(indices.reshape(NX * NZ, KDEV), *grads, columns)

    along_z = lax.all_to_all(values, "z", split_axis=0, concat_axis=0, tiled=True)
    half = jnp.sum(along_z, axis=0) * SCALE
    sent = jnp.broadcast_to(half[None], (ex_size, NX, 2, KDEV)).reshape(ex_size * NX, 2, KDEV)
    received = lax.all_to_all(sent, ex + ("x",), split_axis=0, concat_axis=0, tiled=True)
    raw = jnp.sum(received.reshape(ex_size, NX, 2, KDEV), axis=1)
    own_raw = lax.dynamic_index_in_dim(raw, lax.axis_index(ex), axis=0, keepdims=False)
    return own_raw - jnp.sum(raw, axis=(0, 1))[None, :] / (2 * ex_size)


def solution(mesh):
    grid = Mesh(mesh.devices.reshape(-1, 2, NX, NZ), ("y", "core", "x", "z"))
    ex, par = ("y", "core"), ("x", "z")
    return jax.shard_map(
        shards,
        mesh=grid,
        in_specs=(P(ex, None, par), P(ex, None, par), P(None, par), P()),
        out_specs=P(ex, par),
        check_vma=False,
    )
```

```python
import jax
import jax.numpy as jnp
from jax import lax
from jax.experimental import pallas as pl
from jax.experimental.pallas import tpu as pltpu
from jax.sharding import Mesh, PartitionSpec as P

D = 4096
FF = 16384
TOK = 512
NX = 4
NZ = 16
ROWS = D // NX
COLS = 256
LOW = 64
TILES = ROWS // LOW
KDEV = 128
SAMPLES = NX * KDEV
WIRE = 131072.0
SCALE = 1.0 / 8192.0 / WIRE
VMEM_BYTES = 20 * 1024 * 1024


def sign_of(bits):
    bits = bits ^ (bits >> 4)
    bits = bits ^ (bits >> 2)
    bits = bits ^ (bits >> 1)
    return (1 - 2 * (bits & 1)).astype(jnp.float32)


def split(values):
    high = values.astype(jnp.bfloat16)
    return high, (values - high.astype(jnp.float32)).astype(jnp.bfloat16)


def pack_kernel(acts_in, words_in, out, acts, words, packed, in_sem, act_sem, byte_sem):
    word_copy = pltpu.make_async_copy(words_in, words, in_sem.at[2])
    word_copy.start()
    act_copies = []
    for example in range(2):
        target = acts.at[pl.ds(example * TOK, TOK)]
        act_copies.append(pltpu.make_async_copy(acts_in.at[example], target, in_sem.at[example]))
        act_copies[-1].start()
    copies = []
    for copy in act_copies:
        copy.wait()
    for target in range(NX):
        head = out.at[target, pl.ds(0, 2 * TOK)]
        copies.append(pltpu.make_async_copy(acts, head, act_sem.at[target]))
        copies[-1].start()
    word_copy.wait()
    for target in range(NX):
        word = words[:, target * ROWS : (target + 1) * ROWS]
        two = jnp.concatenate([word & 255, (word >> 8) & 255], axis=0)
        two = two.astype(jnp.float32).astype(jnp.bfloat16)
        for q in range(4):
            packed[target, pl.ds(32 * q, 32), :] = two[:, q * COLS : (q + 1) * COLS]
        tail = out.at[target, pl.ds(2 * TOK, 128)]
        copies.append(pltpu.make_async_copy(packed.at[target], tail, byte_sem.at[target]))
        copies[-1].start()
    for copy in copies:
        copy.wait()


def main_kernel(idx_ref, grads_0, grads_1, columns, out_ref, signs, tiles):
    x, z = lax.axis_index("x"), lax.axis_index("z")

    row = lax.broadcasted_iota(jnp.int32, (COLS, COLS), 0)
    col = lax.broadcasted_iota(jnp.int32, (COLS, COLS), 1)
    had = sign_of(row & col).astype(jnp.bfloat16)
    had = jnp.concatenate([had, had], axis=1)
    byte_row = lax.broadcasted_iota(jnp.int32, (32, COLS), 0)
    byte_col = lax.broadcasted_iota(jnp.int32, (32, COLS), 1)
    chosen_byte = byte_row == (byte_col >> 4) + 16 * ((byte_col >> 3) & 1)
    spread = jnp.where(chosen_byte, 128 >> (byte_col & 7), 0).astype(jnp.float32)
    spread = spread.astype(jnp.bfloat16)

    for block in range(NX):
        for q in range(4):
            two = columns[block, pl.ds(2 * TOK + 32 * q, 32), :]
            value = lax.dot_general(
                two, spread, (((0,), (0,)), ((), ())), preferred_element_type=jnp.float32
            )
            bit = (value.astype(jnp.int32) & 128).astype(jnp.float32)
            signs[block, pl.ds(q * COLS, COLS), :] = 1.0 - bit * (1.0 / 64.0)
        for example, grads in enumerate((grads_0, grads_1)):
            act = columns[block, pl.ds(example * TOK, TOK), :]
            rows = jnp.concatenate([grads[piece] for piece in range(4)], axis=1)
            grad = jnp.dot(rows, act, preferred_element_type=jnp.float32)
            signed = grad * signs[block]
            both = jnp.concatenate(
                [
                    jnp.concatenate(split(signed[b * COLS : (b + 1) * COLS]), axis=0)
                    for b in range(4)
                ],
                axis=1,
            )
            product = jnp.dot(had, both, preferred_element_type=jnp.float32)
            parts = [product[:, b * COLS : (b + 1) * COLS] for b in range(4)]
            p0_, p1_ = parts[0] + parts[1], parts[0] - parts[1]
            p2_, p3_ = parts[2] + parts[3], parts[2] - parts[3]
            for a, value in enumerate((p0_ + p2_, p1_ + p3_, p0_ - p2_, p1_ - p3_)):
                value = value.astype(jnp.bfloat16)
                for i in range(4):
                    tiles[4 * a + i, example, block] = value[i * LOW : (i + 1) * LOW]

    def tile_body(tile, carry):
        idx = jnp.concatenate([idx_ref[pl.ds(tx * NZ + tile, 1), :] for tx in range(NX)], axis=1)
        line = lax.broadcasted_iota(jnp.int32, (16, SAMPLES), 0)
        low_signs = sign_of(line & idx).astype(jnp.bfloat16)
        high_signs = sign_of(line & (idx >> 4)).astype(jnp.bfloat16)
        weights = jnp.concatenate(
            [low_signs * high_signs[a : a + 1] for a in range(16)], axis=0
        )
        sign_xz = sign_of(((idx >> 8) & 15 & z) | (((idx >> 24) & 3 & x) << 4))
        sign_1 = sign_of((idx >> 12) & 1)
        sign_2 = sign_of((idx >> 13) & 1)
        chosen = lax.broadcasted_iota(jnp.int32, (LOW, SAMPLES), 0) == ((idx >> 14) & (LOW - 1))
        left = tiles[tile].reshape(2 * NX * LOW, COLS)
        both = jnp.dot(left, weights, preferred_element_type=jnp.float32)
        for example in range(2):
            b0, b1, b2, b3 = [
                both[(example * NX + j) * LOW : (example * NX + j + 1) * LOW] for j in range(NX)
            ]
            total = (b0 + b1 * sign_1) + (b2 + b3 * sign_1) * sign_2
            picked = jnp.sum(jnp.where(chosen, total, 0.0), axis=0, keepdims=True) * sign_xz
            for tx in range(NX):
                out_ref[tile, tx, pl.ds(example, 1), :] = picked[:, tx * KDEV : (tx + 1) * KDEV]
        return carry

    lax.fori_loop(0, TILES, tile_body, 0, unroll=8)


def shards(activations, out_grads, sign_words, indices):
    ex = ("y", "core")
    ex_size = lax.axis_size(ex)
    vmem = pl.BlockSpec(memory_space=pltpu.VMEM)
    hbm = pl.BlockSpec(memory_space=pltpu.HBM)
    packed = pl.pallas_call(
        pack_kernel,
        out_shape=jax.ShapeDtypeStruct((NX, 2 * TOK + 128, COLS), jnp.bfloat16),
        in_specs=[hbm] * 2,
        out_specs=hbm,
        scratch_shapes=[
            pltpu.VMEM((2 * TOK, COLS), jnp.bfloat16),
            pltpu.VMEM((FF // 1024, D), jnp.int32),
            pltpu.VMEM((NX, 128, COLS), jnp.bfloat16),
            pltpu.SemaphoreType.DMA((3,)),
            pltpu.SemaphoreType.DMA((NX,)),
            pltpu.SemaphoreType.DMA((NX,)),
        ],
        compiler_params=pltpu.CompilerParams(vmem_limit_bytes=60 * 1024 * 1024),
        name="pack_columns_and_words",
    )(activations, jnp.transpose(sign_words, (1, 0)))
    columns = lax.all_to_all(packed, "x", split_axis=0, concat_axis=0, tiled=True)

    wire = jnp.transpose(out_grads, (0, 2, 1)).reshape(2, LOW, 4, KDEV).transpose(0, 2, 1, 3)
    wire = (wire.astype(jnp.float32) * WIRE).astype(jnp.float16)
    wire = lax.all_gather(wire, "z", axis=2, tiled=True)
    grads = [wire[example].astype(jnp.float32).astype(jnp.bfloat16) for example in range(2)]

    values = pl.pallas_call(
        main_kernel,
        out_shape=jax.ShapeDtypeStruct((TILES, NX, 2, KDEV), jnp.float32),
        in_specs=[vmem] * 4,
        out_specs=vmem,
        scratch_shapes=[
            pltpu.VMEM((NX, ROWS, COLS), jnp.float32),
            pltpu.VMEM((TILES, 2, NX, LOW, COLS), jnp.bfloat16),
        ],
        compiler_params=pltpu.CompilerParams(
            vmem_limit_bytes=VMEM_BYTES, allow_input_fusion=[False, True, True, False]
        ),
        cost_estimate=pl.CostEstimate(
            flops=7 * 10**9, bytes_accessed=8 * 1024 * 1024, transcendentals=0
        ),
        name="gradient_transform_sample",
    )(indices.reshape(NX * NZ, KDEV), *grads, columns)

    along_z = lax.all_to_all(values, "z", split_axis=0, concat_axis=0, tiled=True)
    half = jnp.sum(along_z, axis=0) * SCALE
    sent = jnp.broadcast_to(half[None], (ex_size, NX, 2, KDEV)).reshape(ex_size * NX, 2, KDEV)
    received = lax.all_to_all(sent, ex + ("x",), split_axis=0, concat_axis=0, tiled=True)
    raw = jnp.sum(received.reshape(ex_size, NX, 2, KDEV), axis=1)
    own_raw = lax.dynamic_index_in_dim(raw, lax.axis_index(ex), axis=0, keepdims=False)
    return own_raw - jnp.sum(raw, axis=(0, 1))[None, :] / (2 * ex_size)


def solution(mesh):
    grid = Mesh(mesh.devices.reshape(-1, 2, NX, NZ), ("y", "core", "x", "z"))
    ex, par = ("y", "core"), ("x", "z")
    return jax.shard_map(
        shards,
        mesh=grid,
        in_specs=(P(ex, None, par), P(ex, None, par), P(None, par), P()),
        out_specs=P(ex, par),
        check_vma=False,
    )
```

```python
import jax
import jax.numpy as jnp
from jax import lax
from jax.experimental import pallas as pl
from jax.experimental.pallas import tpu as pltpu
from jax.sharding import Mesh, PartitionSpec as P

D = 4096
FF = 16384
TOK = 512
NX = 4
NZ = 16
ROWS = D // NX
COLS = 256
LOW = 64
TILES = ROWS // LOW
KDEV = 128
SAMPLES = NX * KDEV
WIRE = 131072.0
SCALE = 1.0 / 8192.0 / WIRE
VMEM_BYTES = 20 * 1024 * 1024


def sign_of(bits):
    bits = bits ^ (bits >> 4)
    bits = bits ^ (bits >> 2)
    bits = bits ^ (bits >> 1)
    return (1 - 2 * (bits & 1)).astype(jnp.float32)


def split(values):
    high = values.astype(jnp.bfloat16)
    return high, (values - high.astype(jnp.float32)).astype(jnp.bfloat16)


def pack_kernel(acts_in, words_in, out, acts, words, packed, in_sem, act_sem, byte_sem):
    word_copy = pltpu.make_async_copy(words_in, words, in_sem.at[2])
    word_copy.start()
    act_copies = []
    for example in range(2):
        target = acts.at[pl.ds(example * TOK, TOK)]
        act_copies.append(pltpu.make_async_copy(acts_in.at[example], target, in_sem.at[example]))
        act_copies[-1].start()
    copies = []
    for copy in act_copies:
        copy.wait()
    for target in range(NX):
        head = out.at[target, pl.ds(0, 2 * TOK)]
        copies.append(pltpu.make_async_copy(acts, head, act_sem.at[target]))
        copies[-1].start()
    word_copy.wait()
    for target in range(NX):
        word = words[:, target * ROWS : (target + 1) * ROWS]
        two = jnp.concatenate([word & 255, (word >> 8) & 255], axis=0)
        two = two.astype(jnp.float32).astype(jnp.bfloat16)
        for q in range(4):
            packed[target, pl.ds(32 * q, 32), :] = two[:, q * COLS : (q + 1) * COLS]
        tail = out.at[target, pl.ds(2 * TOK, 128)]
        copies.append(pltpu.make_async_copy(packed.at[target], tail, byte_sem.at[target]))
        copies[-1].start()
    for copy in copies:
        copy.wait()


def main_kernel(idx_ref, grads_0, grads_1, columns, out_ref, signs, tiles):
    x, z = lax.axis_index("x"), lax.axis_index("z")
    core = lax.axis_index("core")

    row = lax.broadcasted_iota(jnp.int32, (COLS, COLS), 0)
    col = lax.broadcasted_iota(jnp.int32, (COLS, COLS), 1)
    had = sign_of(row & col).astype(jnp.bfloat16)
    had = jnp.concatenate([had, had], axis=1)
    byte_row = lax.broadcasted_iota(jnp.int32, (32, COLS), 0)
    byte_col = lax.broadcasted_iota(jnp.int32, (32, COLS), 1)
    chosen_byte = byte_row == (byte_col >> 4) + 16 * ((byte_col >> 3) & 1)
    spread = jnp.where(chosen_byte, 128 >> (byte_col & 7), 0).astype(jnp.float32)
    spread = spread.astype(jnp.bfloat16)

    for block in range(NX):
        for q in range(4):
            start = pl.multiple_of(2 * TOK + 32 * (q ^ (2 * core)), 32)
            two = columns[block, pl.ds(start, 32), :]
            value = lax.dot_general(
                two, spread, (((0,), (0,)), ((), ())), preferred_element_type=jnp.float32
            )
            bit = (value.astype(jnp.int32) & 128).astype(jnp.float32)
            signs[block, pl.ds(q * COLS, COLS), :] = 1.0 - bit * (1.0 / 64.0)
        for example, grads in enumerate((grads_0, grads_1)):
            act = columns[block, pl.ds(example * TOK, TOK), :]
            grad = jnp.dot(grads[...], act, preferred_element_type=jnp.float32)
            signed = grad * signs[block]
            parts = []
            for b in range(4):
                both = jnp.concatenate(split(signed[b * COLS : (b + 1) * COLS]), axis=0)
                parts.append(jnp.dot(had, both, preferred_element_type=jnp.float32))
            p0_, p1_ = parts[0] + parts[1], parts[0] - parts[1]
            p2_, p3_ = parts[2] + parts[3], parts[2] - parts[3]
            for a, value in enumerate((p0_ + p2_, p1_ + p3_, p0_ - p2_, p1_ - p3_)):
                value = value.astype(jnp.bfloat16)
                for i in range(4):
                    tiles[4 * a + i, example, block] = value[i * LOW : (i + 1) * LOW]

    def tile_body(tile, carry):
        idx = jnp.concatenate([idx_ref[pl.ds(tx * NZ + tile, 1), :] for tx in range(NX)], axis=1)
        line = lax.broadcasted_iota(jnp.int32, (16, SAMPLES), 0)
        low_signs = sign_of(line & idx).astype(jnp.bfloat16)
        high_signs = sign_of(line & (idx >> 4)).astype(jnp.bfloat16)
        weights = jnp.concatenate(
            [low_signs * high_signs[a : a + 1] for a in range(16)], axis=0
        )
        swap = (tile >> 3) & core
        sign_xz = sign_of(((idx >> 8) & 15 & z) | (((idx >> 24) & 3 & x) << 4) | (swap << 6))
        sign_1 = sign_of((idx >> 12) & 1)
        sign_2 = sign_of((idx >> 13) & 1)
        chosen = lax.broadcasted_iota(jnp.int32, (LOW, SAMPLES), 0) == ((idx >> 14) & (LOW - 1))
        left = tiles[tile].reshape(2 * NX * LOW, COLS)
        both = jnp.dot(left, weights, preferred_element_type=jnp.float32)
        for example in range(2):
            b0, b1, b2, b3 = [
                both[(example * NX + j) * LOW : (example * NX + j + 1) * LOW] for j in range(NX)
            ]
            total = (b0 + b1 * sign_1) + (b2 + b3 * sign_1) * sign_2
            picked = jnp.sum(jnp.where(chosen, total, 0.0), axis=0, keepdims=True) * sign_xz
            for tx in range(NX):
                out_ref[tile, tx, pl.ds(example, 1), :] = picked[:, tx * KDEV : (tx + 1) * KDEV]
        return carry

    lax.fori_loop(0, TILES, tile_body, 0, unroll=8)


def shards(activations, out_grads, sign_words, indices):
    ex = ("y", "core")
    ex_size = lax.axis_size(ex)
    vmem = pl.BlockSpec(memory_space=pltpu.VMEM)
    hbm = pl.BlockSpec(memory_space=pltpu.HBM)
    packed = pl.pallas_call(
        pack_kernel,
        out_shape=jax.ShapeDtypeStruct((NX, 2 * TOK + 128, COLS), jnp.bfloat16),
        in_specs=[hbm] * 2,
        out_specs=hbm,
        scratch_shapes=[
            pltpu.VMEM((2 * TOK, COLS), jnp.bfloat16),
            pltpu.VMEM((FF // 1024, D), jnp.int32),
            pltpu.VMEM((NX, 128, COLS), jnp.bfloat16),
            pltpu.SemaphoreType.DMA((3,)),
            pltpu.SemaphoreType.DMA((NX,)),
            pltpu.SemaphoreType.DMA((NX,)),
        ],
        compiler_params=pltpu.CompilerParams(vmem_limit_bytes=60 * 1024 * 1024),
        name="pack_columns_and_words",
    )(activations, jnp.transpose(sign_words, (1, 0)))
    columns = lax.all_to_all(packed, "x", split_axis=0, concat_axis=0, tiled=True)

    wire = jnp.transpose(out_grads, (0, 2, 1)).astype(jnp.float32) * WIRE
    wire = lax.all_gather(
        wire.astype(jnp.float16), ("core", "z"), axis=1, tiled=True,
        axis_index_groups=[list(range(NZ)), [NZ + (i ^ 8) for i in range(NZ)]],
    )
    grads = [wire[example].astype(jnp.float32).astype(jnp.bfloat16) for example in range(2)]

    values = pl.pallas_call(
        main_kernel,
        out_shape=jax.ShapeDtypeStruct((TILES, NX, 2, KDEV), jnp.float32),
        in_specs=[vmem] * 4,
        out_specs=vmem,
        scratch_shapes=[
            pltpu.VMEM((NX, ROWS, COLS), jnp.float32),
            pltpu.VMEM((TILES, 2, NX, LOW, COLS), jnp.bfloat16),
        ],
        compiler_params=pltpu.CompilerParams(
            vmem_limit_bytes=VMEM_BYTES, allow_input_fusion=[False, True, True, False]
        ),
        cost_estimate=pl.CostEstimate(
            flops=7 * 10**9, bytes_accessed=8 * 1024 * 1024, transcendentals=0
        ),
        name="gradient_transform_sample",
    )(indices.reshape(NX * NZ, KDEV), *grads, columns)

    along_z = lax.all_to_all(values, "z", split_axis=0, concat_axis=0, tiled=True)
    half = jnp.sum(along_z, axis=0) * SCALE
    sent = jnp.broadcast_to(half[None], (ex_size, NX, 2, KDEV)).reshape(ex_size * NX, 2, KDEV)
    received = lax.all_to_all(sent, ex + ("x",), split_axis=0, concat_axis=0, tiled=True)
    raw = jnp.sum(received.reshape(ex_size, NX, 2, KDEV), axis=1)
    own_raw = lax.dynamic_index_in_dim(raw, lax.axis_index(ex), axis=0, keepdims=False)
    return own_raw - jnp.sum(raw, axis=(0, 1))[None, :] / (2 * ex_size)


def solution(mesh):
    grid = Mesh(mesh.devices.reshape(-1, 2, NX, NZ), ("y", "core", "x", "z"))
    ex, par = ("y", "core"), ("x", "z")
    return jax.shard_map(
        shards,
        mesh=grid,
        in_specs=(P(ex, None, par), P(ex, None, par), P(None, par), P()),
        out_specs=P(ex, par),
        check_vma=False,
    )
```

```python
import jax
import jax.numpy as jnp
from jax import lax
from jax.experimental import pallas as pl
from jax.experimental.pallas import tpu as pltpu
from jax.sharding import Mesh, PartitionSpec as P

D = 4096
FF = 16384
TOK = 512
NX = 4
NZ = 16
ROWS = D // NX
COLS = 256
LOW = 64
TILES = ROWS // LOW
KDEV = 128
SAMPLES = NX * KDEV
WIRE = 131072.0
SCALE = 1.0 / 8192.0 / WIRE
VMEM_BYTES = 20 * 1024 * 1024


def sign_of(bits):
    bits = bits ^ (bits >> 4)
    bits = bits ^ (bits >> 2)
    bits = bits ^ (bits >> 1)
    return (1 - 2 * (bits & 1)).astype(jnp.float32)


def split(values):
    high = values.astype(jnp.bfloat16)
    return high, (values - high.astype(jnp.float32)).astype(jnp.bfloat16)


def pack_kernel(acts_in, words_in, out, acts, words, packed, in_sem, act_sem, byte_sem):
    word_copy = pltpu.make_async_copy(words_in, words, in_sem.at[2])
    word_copy.start()
    act_copies = []
    for example in range(2):
        target = acts.at[pl.ds(example * TOK, TOK)]
        act_copies.append(pltpu.make_async_copy(acts_in.at[example], target, in_sem.at[example]))
        act_copies[-1].start()
    copies = []
    for copy in act_copies:
        copy.wait()
    for target in range(NX):
        for piece in range(4):
            rows = pl.ds(piece * COLS, COLS)
            copy = pltpu.make_async_copy(
                acts.at[rows], out.at[target, rows], act_sem.at[target, piece]
            )
            copy.start()
            copies.append(copy)
    word_copy.wait()
    for target in range(NX):
        word = words[:, target * ROWS : (target + 1) * ROWS]
        two = jnp.concatenate([word & 255, (word >> 8) & 255], axis=0)
        two = two.astype(jnp.float32).astype(jnp.bfloat16)
        for q in range(4):
            packed[target, pl.ds(32 * q, 32), :] = two[:, q * COLS : (q + 1) * COLS]
        tail = out.at[target, pl.ds(2 * TOK, 128)]
        copies.append(pltpu.make_async_copy(packed.at[target], tail, byte_sem.at[target]))
        copies[-1].start()
    for copy in copies:
        copy.wait()


def main_kernel(idx_ref, grads_0, grads_1, columns, out_ref, signs, tiles):
    z = lax.axis_index("z")

    row = lax.broadcasted_iota(jnp.int32, (COLS, COLS), 0)
    col = lax.broadcasted_iota(jnp.int32, (COLS, COLS), 1)
    had = sign_of(row & col).astype(jnp.bfloat16)
    had = jnp.concatenate([had, had], axis=1)
    byte_row = lax.broadcasted_iota(jnp.int32, (32, COLS), 0)
    byte_col = lax.broadcasted_iota(jnp.int32, (32, COLS), 1)
    chosen_byte = byte_row == (byte_col >> 4) + 16 * ((byte_col >> 3) & 1)
    spread = jnp.where(chosen_byte, 128 >> (byte_col & 7), 0).astype(jnp.float32)
    spread = spread.astype(jnp.bfloat16)

    for block in range(NX):
        for q in range(4):
            two = columns[block, pl.ds(2 * TOK + 32 * q, 32), :]
            value = lax.dot_general(
                two, spread, (((0,), (0,)), ((), ())), preferred_element_type=jnp.float32
            )
            bit = (value.astype(jnp.int32) & 128).astype(jnp.float32)
            signs[block, pl.ds(q * COLS, COLS), :] = 1.0 - bit * (1.0 / 64.0)
        for example, grads in enumerate((grads_0, grads_1)):
            act = columns[block, pl.ds(example * TOK, TOK), :]
            grad = jnp.dot(grads[...], act, preferred_element_type=jnp.float32)
            signed = grad * signs[block]
            parts = []
            for b in range(4):
                both = jnp.concatenate(split(signed[b * COLS : (b + 1) * COLS]), axis=0)
                parts.append(jnp.dot(had, both, preferred_element_type=jnp.float32))
            p0_, p1_ = parts[0] + parts[1], parts[0] - parts[1]
            p2_, p3_ = parts[2] + parts[3], parts[2] - parts[3]
            for a, value in enumerate((p0_ + p2_, p1_ + p3_, p0_ - p2_, p1_ - p3_)):
                value = value.astype(jnp.bfloat16)
                for i in range(4):
                    tiles[4 * a + i, example, block] = value[i * LOW : (i + 1) * LOW]

    def tile_body(tile, carry):
        idx = jnp.concatenate([idx_ref[pl.ds(tx * NZ + tile, 1), :] for tx in range(NX)], axis=1)
        line = lax.broadcasted_iota(jnp.int32, (16, SAMPLES), 0)
        low_signs = sign_of(line & idx).astype(jnp.bfloat16)
        high_signs = sign_of(line & (idx >> 4)).astype(jnp.bfloat16)
        weights = jnp.concatenate(
            [low_signs * high_signs[a : a + 1] for a in range(16)], axis=0
        )
        sign_z = sign_of((idx >> 8) & 15 & z)
        sign_1 = sign_of((idx >> 12) & 1)
        sign_2 = sign_of((idx >> 13) & 1)
        chosen = lax.broadcasted_iota(jnp.int32, (LOW, SAMPLES), 0) == ((idx >> 14) & (LOW - 1))
        left = tiles[tile].reshape(2 * NX * LOW, COLS)
        both = jnp.dot(left, weights, preferred_element_type=jnp.float32)
        for example in range(2):
            b0, b1, b2, b3 = [
                both[(example * NX + j) * LOW : (example * NX + j + 1) * LOW] for j in range(NX)
            ]
            total = (b0 + b1 * sign_1) + (b2 + b3 * sign_1) * sign_2
            picked = jnp.sum(jnp.where(chosen, total, 0.0), axis=0, keepdims=True) * sign_z
            for tx in range(NX):
                out_ref[tile, tx, pl.ds(example, 1), :] = picked[:, tx * KDEV : (tx + 1) * KDEV]
        return carry

    lax.fori_loop(0, TILES, tile_body, 0, unroll=8)


def shards(activations, out_grads, sign_words, indices):
    ex = ("y", "core")
    ex_size = lax.axis_size(ex)
    vmem = pl.BlockSpec(memory_space=pltpu.VMEM)
    hbm = pl.BlockSpec(memory_space=pltpu.HBM)
    packed = pl.pallas_call(
        pack_kernel,
        out_shape=jax.ShapeDtypeStruct((NX, 2 * TOK + 128, COLS), jnp.bfloat16),
        in_specs=[hbm] * 2,
        out_specs=hbm,
        scratch_shapes=[
            pltpu.VMEM((2 * TOK, COLS), jnp.bfloat16),
            pltpu.VMEM((FF // 1024, D), jnp.int32),
            pltpu.VMEM((NX, 128, COLS), jnp.bfloat16),
            pltpu.SemaphoreType.DMA((3,)),
            pltpu.SemaphoreType.DMA((NX, 4)),
            pltpu.SemaphoreType.DMA((NX,)),
        ],
        compiler_params=pltpu.CompilerParams(vmem_limit_bytes=60 * 1024 * 1024),
        name="pack_columns_and_words",
    )(activations, jnp.transpose(sign_words, (1, 0)))
    columns = lax.all_to_all(packed, "x", split_axis=0, concat_axis=0, tiled=True)

    wire = jnp.transpose(out_grads, (0, 2, 1)).astype(jnp.float32) * WIRE
    wire = lax.all_gather(wire.astype(jnp.float16), "z", axis=1, tiled=True)
    grads = [wire[example].astype(jnp.float32).astype(jnp.bfloat16) for example in range(2)]

    values = pl.pallas_call(
        main_kernel,
        out_shape=jax.ShapeDtypeStruct((TILES, NX, 2, KDEV), jnp.float32),
        in_specs=[vmem] * 4,
        out_specs=vmem,
        scratch_shapes=[
            pltpu.VMEM((NX, ROWS, COLS), jnp.float32),
            pltpu.VMEM((TILES, 2, NX, LOW, COLS), jnp.bfloat16),
        ],
        compiler_params=pltpu.CompilerParams(
            vmem_limit_bytes=VMEM_BYTES, allow_input_fusion=[False, True, True, False]
        ),
        cost_estimate=pl.CostEstimate(
            flops=7 * 10**9, bytes_accessed=8 * 1024 * 1024, transcendentals=0
        ),
        name="gradient_transform_sample",
    )(indices.reshape(NX * NZ, KDEV), *grads, columns)

    along_z = lax.all_to_all(values, "z", split_axis=0, concat_axis=0, tiled=True)
    own_indices = lax.dynamic_index_in_dim(
        indices.reshape(NX, NZ, KDEV), lax.axis_index("z"), axis=1, keepdims=False
    )
    own_signs = sign_of((own_indices >> 24) & lax.axis_index("x")) * SCALE
    half = jnp.sum(along_z, axis=0) * own_signs[:, None, :]
    sent = jnp.broadcast_to(half[None], (ex_size, NX, 2, KDEV)).reshape(ex_size * NX, 2, KDEV)
    received = lax.all_to_all(sent, ex + ("x",), split_axis=0, concat_axis=0, tiled=True)
    raw = jnp.sum(received.reshape(ex_size, NX, 2, KDEV), axis=1)
    own_raw = lax.dynamic_index_in_dim(raw, lax.axis_index(ex), axis=0, keepdims=False)
    return own_raw - jnp.sum(raw, axis=(0, 1))[None, :] / (2 * ex_size)


def solution(mesh):
    grid = Mesh(mesh.devices.reshape(-1, 2, NX, NZ), ("y", "core", "x", "z"))
    ex, par = ("y", "core"), ("x", "z")
    return jax.shard_map(
        shards,
        mesh=grid,
        in_specs=(P(ex, None, par), P(ex, None, par), P(None, par), P()),
        out_specs=P(ex, par),
        check_vma=False,
    )
```

```python
import jax
import jax.numpy as jnp
from jax import lax
from jax.experimental import pallas as pl
from jax.experimental.pallas import tpu as pltpu
from jax.sharding import Mesh, PartitionSpec as P

D = 4096
FF = 16384
TOK = 512
NX = 4
NZ = 16
ROWS = D // NX
COLS = 256
LOW = 64
TILES = ROWS // LOW
KDEV = 128
SAMPLES = NX * KDEV
WIRE = 131072.0
SCALE = 1.0 / 8192.0 / WIRE
VMEM_BYTES = 20 * 1024 * 1024


def sign_of(bits):
    bits = bits ^ (bits >> 4)
    bits = bits ^ (bits >> 2)
    bits = bits ^ (bits >> 1)
    return (1 - 2 * (bits & 1)).astype(jnp.float32)


def split(values):
    high = values.astype(jnp.bfloat16)
    return high, (values - high.astype(jnp.float32)).astype(jnp.bfloat16)


def pack_kernel(acts_in, words_in, out, acts, words, packed, in_sem, act_sem, byte_sem):
    word_copy = pltpu.make_async_copy(words_in, words, in_sem.at[2])
    word_copy.start()
    act_copies = []
    for example in range(2):
        target = acts.at[pl.ds(example * TOK, TOK)]
        act_copies.append(pltpu.make_async_copy(acts_in.at[example], target, in_sem.at[example]))
        act_copies[-1].start()
    copies = []
    for copy in act_copies:
        copy.wait()
    for target in range(NX):
        head = out.at[target, pl.ds(0, 2 * TOK)]
        copies.append(pltpu.make_async_copy(acts, head, act_sem.at[target]))
        copies[-1].start()
    word_copy.wait()
    for target in range(NX):
        word = words[:, target * ROWS : (target + 1) * ROWS]
        two = jnp.concatenate([word & 255, (word >> 8) & 255], axis=0)
        two = two.astype(jnp.float32).astype(jnp.bfloat16)
        for q in range(4):
            packed[target, pl.ds(32 * q, 32), :] = two[:, q * COLS : (q + 1) * COLS]
        tail = out.at[target, pl.ds(2 * TOK, 128)]
        copies.append(pltpu.make_async_copy(packed.at[target], tail, byte_sem.at[target]))
        copies[-1].start()
    for copy in copies:
        copy.wait()


def main_kernel(idx_ref, grads_0, grads_1, columns, out_ref, tiles):
    x, z = lax.axis_index("x"), lax.axis_index("z")

    row = lax.broadcasted_iota(jnp.int32, (COLS, COLS), 0)
    col = lax.broadcasted_iota(jnp.int32, (COLS, COLS), 1)
    had = sign_of(row & col).astype(jnp.bfloat16)
    had = jnp.concatenate([had, had], axis=1)
    byte_row = lax.broadcasted_iota(jnp.int32, (32, COLS), 0)
    byte_col = lax.broadcasted_iota(jnp.int32, (32, COLS), 1)
    chosen_byte = byte_row == (byte_col >> 4) + 16 * ((byte_col >> 3) & 1)
    spread = jnp.where(chosen_byte, 128 >> (byte_col & 7), 0).astype(jnp.float32)
    spread = spread.astype(jnp.bfloat16)

    for block in range(NX):
        chunks = []
        for q in range(4):
            two = columns[block, pl.ds(2 * TOK + 32 * q, 32), :]
            value = lax.dot_general(
                two, spread, (((0,), (0,)), ((), ())), preferred_element_type=jnp.float32
            )
            bit = (value.astype(jnp.int32) & 128).astype(jnp.float32)
            chunks.append(1.0 - bit * (1.0 / 64.0))
        signs = jnp.concatenate(chunks, axis=0)
        for example, grads in enumerate((grads_0, grads_1)):
            act = columns[block, pl.ds(example * TOK, TOK), :]
            grad = jnp.dot(grads[...], act, preferred_element_type=jnp.float32)
            signed = grad * signs
            parts = []
            for b in range(4):
                both = jnp.concatenate(split(signed[b * COLS : (b + 1) * COLS]), axis=0)
                parts.append(jnp.dot(had, both, preferred_element_type=jnp.float32))
            p0_, p1_ = parts[0] + parts[1], parts[0] - parts[1]
            p2_, p3_ = parts[2] + parts[3], parts[2] - parts[3]
            for a, value in enumerate((p0_ + p2_, p1_ + p3_, p0_ - p2_, p1_ - p3_)):
                value = value.astype(jnp.bfloat16)
                for i in range(4):
                    tiles[4 * a + i, example, block] = value[i * LOW : (i + 1) * LOW]

    def tile_body(tile, carry):
        idx = jnp.concatenate([idx_ref[pl.ds(tx * NZ + tile, 1), :] for tx in range(NX)], axis=1)
        line = lax.broadcasted_iota(jnp.int32, (16, SAMPLES), 0)
        low_signs = sign_of(line & idx).astype(jnp.bfloat16)
        high_signs = sign_of(line & (idx >> 4)).astype(jnp.bfloat16)
        weights = jnp.concatenate(
            [low_signs * high_signs[a : a + 1] for a in range(16)], axis=0
        )
        sign_xz = sign_of(((idx >> 8) & 15 & z) | (((idx >> 24) & 3 & x) << 4))
        sign_1 = sign_of((idx >> 12) & 1)
        sign_2 = sign_of((idx >> 13) & 1)
        chosen = lax.broadcasted_iota(jnp.int32, (LOW, SAMPLES), 0) == ((idx >> 14) & (LOW - 1))
        left = tiles[tile].reshape(2 * NX * LOW, COLS)
        both = jnp.dot(left, weights, preferred_element_type=jnp.float32)
        for example in range(2):
            b0, b1, b2, b3 = [
                both[(example * NX + j) * LOW : (example * NX + j + 1) * LOW] for j in range(NX)
            ]
            total = (b0 + b1 * sign_1) + (b2 + b3 * sign_1) * sign_2
            picked = jnp.sum(jnp.where(chosen, total, 0.0), axis=0, keepdims=True) * sign_xz
            for tx in range(NX):
                out_ref[tile, tx, pl.ds(example, 1), :] = picked[:, tx * KDEV : (tx + 1) * KDEV]
        return carry

    lax.fori_loop(0, TILES, tile_body, 0, unroll=8)


def shards(activations, out_grads, sign_words, indices):
    ex = ("y", "core")
    ex_size = lax.axis_size(ex)
    vmem = pl.BlockSpec(memory_space=pltpu.VMEM)
    hbm = pl.BlockSpec(memory_space=pltpu.HBM)
    packed = pl.pallas_call(
        pack_kernel,
        out_shape=jax.ShapeDtypeStruct((NX, 2 * TOK + 128, COLS), jnp.bfloat16),
        in_specs=[hbm] * 2,
        out_specs=hbm,
        scratch_shapes=[
            pltpu.VMEM((2 * TOK, COLS), jnp.bfloat16),
            pltpu.VMEM((FF // 1024, D), jnp.int32),
            pltpu.VMEM((NX, 128, COLS), jnp.bfloat16),
            pltpu.SemaphoreType.DMA((3,)),
            pltpu.SemaphoreType.DMA((NX,)),
            pltpu.SemaphoreType.DMA((NX,)),
        ],
        compiler_params=pltpu.CompilerParams(vmem_limit_bytes=60 * 1024 * 1024),
        name="pack_columns_and_words",
    )(activations, jnp.transpose(sign_words, (1, 0)))
    columns = lax.all_to_all(packed, "x", split_axis=0, concat_axis=0, tiled=True)

    wire = jnp.transpose(out_grads, (0, 2, 1)).astype(jnp.float32) * WIRE
    wire = lax.all_gather(wire.astype(jnp.float16), "z", axis=1, tiled=True)
    grads = [wire[example].astype(jnp.float32).astype(jnp.bfloat16) for example in range(2)]

    values = pl.pallas_call(
        main_kernel,
        out_shape=jax.ShapeDtypeStruct((TILES, NX, 2, KDEV), jnp.float32),
        in_specs=[vmem] * 4,
        out_specs=vmem,
        scratch_shapes=[
            pltpu.VMEM((TILES, 2, NX, LOW, COLS), jnp.bfloat16),
        ],
        compiler_params=pltpu.CompilerParams(
            vmem_limit_bytes=VMEM_BYTES, allow_input_fusion=[False, True, True, False]
        ),
        cost_estimate=pl.CostEstimate(
            flops=7 * 10**9, bytes_accessed=8 * 1024 * 1024, transcendentals=0
        ),
        name="gradient_transform_sample",
    )(indices.reshape(NX * NZ, KDEV), *grads, columns)

    along_z = lax.all_to_all(values, "z", split_axis=0, concat_axis=0, tiled=True)
    half = jnp.sum(along_z, axis=0) * SCALE
    sent = jnp.broadcast_to(half[None], (ex_size, NX, 2, KDEV)).reshape(ex_size * NX, 2, KDEV)
    received = lax.all_to_all(sent, ex + ("x",), split_axis=0, concat_axis=0, tiled=True)
    raw = jnp.sum(received.reshape(ex_size, NX, 2, KDEV), axis=1)
    own_raw = lax.dynamic_index_in_dim(raw, lax.axis_index(ex), axis=0, keepdims=False)
    return own_raw - jnp.sum(raw, axis=(0, 1))[None, :] / (2 * ex_size)


def solution(mesh):
    grid = Mesh(mesh.devices.reshape(-1, 2, NX, NZ), ("y", "core", "x", "z"))
    ex, par = ("y", "core"), ("x", "z")
    return jax.shard_map(
        shards,
        mesh=grid,
        in_specs=(P(ex, None, par), P(ex, None, par), P(None, par), P()),
        out_specs=P(ex, par),
        check_vma=False,
    )
```
